32 devices in a mesh: stretch: 4 (over y, x), seq: 8 (over z, core).
Axes of the slice: x: 2, y: 2, z: 4, core: 2. Of those that a mesh axis runs over, the one named last changes fastest.
Arguments:
- query_rows: bfloat16 [4, 256, 4096], P('stretch', 'seq'), may hold values from -160 to 160
- key_rows: bfloat16 [4, 256, 4096], P('stretch', 'seq'), may hold values from -5 to 5
- value_rows: bfloat16 [4, 256, 4096], P('stretch', 'seq'), may hold values from -6 to 6
- cache_from: int32 [4], P('stretch'), may hold values from 0 to 255
- time_index: int32 [4], P('stretch'), may hold values from 0 to 49
- gate_table: float32 [50, 4096], replicated, may hold values from 4 to 16
Outputs:
- attn_out: bfloat16 [4, 256, 4096], P('stretch', 'seq')
The draws below stay inside these ranges and needn't reach their ends.
All inputs are finite; a program needn't handle non-finite values.
Results may differ from the reference program's by a relative error of at most 0.0055.
Values may be sent and summed in bfloat16 or wider, within the bound.
No kernel may reach another device: no remote copies, remote signals or barrier semaphores. Data moves between devices by JAX's collectives and lax.ppermute only.
A program may use at most 64 MiB of HBM per device.

```python
import math
import jax
import jax.numpy as jnp
from jax import lax

HEADS = 32
HD = 128
FEAT = 4096
TOKENS = 256
CLIPS = 4
NSTEPS = 50


def paired_draw(key):
    base = jax.random.fold_in(key, 17)
    key_draw = jnp.clip(jax.random.normal(jax.random.fold_in(base, 1), (CLIPS, TOKENS, FEAT), jnp.float32), -5.0, 5.0)
    query_draw = jnp.clip(2.0 * jax.random.normal(jax.random.fold_in(base, 2), (CLIPS, TOKENS, FEAT), jnp.float32), -12.0, 12.0)
    return (query_draw, key_draw)


def draw_query_rows(key, part):
    return paired_draw(key)[0].astype(jnp.bfloat16)


def draw_key_rows(key, part):
    return paired_draw(key)[1].astype(jnp.bfloat16)


def with_ends(array, rng, least, high):
    index_at = [jax.random.randint(jax.random.fold_in(rng, axis), (), 0, length) for axis, length in enumerate(array.shape)]
    main_axis = array.shape.index(max(array.shape))
    beside = index_at[:main_axis] + [(index_at[main_axis] + 1) % array.shape[main_axis]] + index_at[main_axis + 1:]
    return array.at[tuple(index_at)].set(least).at[tuple(beside)].set(high)


def levels(stream_key, extent, shards, least, high):
    def one(dim, parts):
        heights = jax.random.uniform(jax.random.fold_in(jax.random.fold_in(stream_key, 6), dim), (parts,), jnp.float32, least / len(shards), high / len(shards))
        return jnp.repeat(jnp.exp(heights), extent[dim] // parts).reshape((-1,) + (1,) * (len(extent) - dim - 1))

    loudness = one(*shards[0])
    for cut in shards[1:]:
        loudness = loudness * one(*cut)
    return loudness


def bell_draw(key, shape, scale, limit, split=(), kind=jnp.bfloat16):
    result = jax.random.normal(key, shape, jnp.float32) * scale
    if len(split) > 0:
        result = levels(key, shape, split, -0.22, 0.18) * result
    return jnp.clip(result, min=-limit, max=limit).astype(kind)


def setup_inputs(seed: int = 0) -> dict:
    key_of = jax.random.split(jax.random.key(seed), 7)
    return {
        "query_rows": draw_query_rows(jax.random.fold_in(key_of[6], 71), 0),
        "key_rows": draw_key_rows(jax.random.fold_in(key_of[6], 71), 0),
        "value_rows": bell_draw(key_of[2], (CLIPS, TOKENS, FEAT), 1.0, 6.0, ((0, 4), (1, 8))),
        "cache_from": with_ends(jax.random.randint(key_of[3], (CLIPS,), 0, TOKENS), jax.random.fold_in(key_of[3], 1), 0, TOKENS - 1).astype(jnp.int32),
        "time_index": with_ends(jax.random.randint(key_of[4], (CLIPS,), 0, NSTEPS), jax.random.fold_in(key_of[4], 1), 0, NSTEPS - 1).astype(jnp.int32),
        "gate_table": jnp.clip(jnp.exp(jax.random.uniform(key_of[5], (NSTEPS, FEAT), jnp.float32, math.log(4.0), math.log(16.0))), 4.0, 16.0),
    }


def attend_head(head_query, head_key, head_value, visible):
    scores = jnp.dot(head_query, head_key.T, preferred_element_type=jnp.float32) * (HD ** -0.5)
    scores = jnp.where(visible[None, :], scores, -1e30)
    largest = jnp.max(scores, axis=1, keepdims=True)
    weights = jnp.where(visible[None, :], jnp.exp(scores - largest), 0.0)
    total = jnp.sum(weights, axis=1, keepdims=True)
    numer = jnp.dot(weights.astype(jnp.bfloat16), head_value, preferred_element_type=jnp.float32)
    return (numer / total).astype(jnp.bfloat16)


def reference(query_rows, key_rows, value_rows, cache_from, time_index, gate_table):
    position = jnp.arange(TOKENS).astype(jnp.int32)
    attn_list = []
    for clip_index in range(CLIPS):
        own_visible = jnp.ones((TOKENS,), bool)
        if clip_index > 0:
            past_key = key_rows[clip_index - 1]
            past_value = value_rows[clip_index - 1]
            past_visible = position >= cache_from[clip_index].astype(jnp.int32)
        else:
            past_key = jnp.zeros_like(key_rows[0])
            past_value = jnp.zeros_like(value_rows[0])
            past_visible = jnp.zeros((TOKENS,), bool)
        visible = jnp.concatenate([own_visible, past_visible])
        keys_all = jnp.concatenate([key_rows[clip_index], past_key], 0).reshape(2 * TOKENS, HEADS, HD).transpose(1, 0, 2)
        values_all = jnp.concatenate([value_rows[clip_index], past_value], 0).reshape(2 * TOKENS, HEADS, HD).transpose(1, 0, 2)
        head_queries = query_rows[clip_index].reshape(TOKENS, HEADS, HD).transpose(1, 0, 2)
        heads_out = lax.map(lambda packed: attend_head(packed[0], packed[1], packed[2], visible), (head_queries, keys_all, values_all))
        attended = heads_out.transpose(1, 0, 2).reshape(TOKENS, FEAT)
        gate_row = gate_table[time_index[clip_index]]
        attn_list.append((attended.astype(jnp.float32) * gate_row).astype(jnp.bfloat16))
    return jnp.stack(attn_list)
```

```python
import math

import jax
import jax.numpy as jnp
from jax import lax
from jax.experimental import pallas as pl
from jax.experimental.pallas import tpu as pltpu
from jax.sharding import PartitionSpec as P

HEADS = 32
HD = 128
VMEM = pl.BlockSpec(memory_space=pltpu.VMEM)
SMEM = pl.BlockSpec(memory_space=pltpu.SMEM)
ANY = pl.BlockSpec(memory_space=pl.ANY)


def passed_along(block, axis, distance):
    devices = range(lax.axis_size(axis))
    route = [(i - distance, i) for i in devices if i - distance in devices]
    return lax.ppermute(block, axis, route)


def spread(rows, groups, per_dev, blocks):
    count = rows.shape[0]
    arranged = rows.reshape(count, groups, per_dev, HD).transpose(1, 0, 2, 3)
    return jnp.repeat(arranged, blocks, axis=0)


def general_body(query_rows, key_rows, value_rows, cache_from, time_index, gate_table):
    seq_count = lax.axis_size("seq")
    own_count = query_rows.shape[1]
    blocks = max(seq_count // HEADS, 1)
    per_dev = HEADS * blocks // seq_count
    groups = HEADS // per_dev
    part_len = own_count // blocks
    queries = query_rows[0].reshape(blocks, part_len, groups, per_dev, HD).transpose(2, 0, 1, 3, 4)
    queries = queries.reshape(groups * blocks, part_len, per_dev, HD)
    got_query, got_key, got_value = (
        lax.all_to_all(queries, "seq", split_axis=0, concat_axis=1, tiled=True),
        lax.all_to_all(
            spread(key_rows[0], groups, per_dev, blocks),
            "seq",
            split_axis=0,
            concat_axis=1,
            tiled=True,
        ),
        lax.all_to_all(
            spread(value_rows[0], groups, per_dev, blocks),
            "seq",
            split_axis=0,
            concat_axis=1,
            tiled=True,
        ),
    )
    got_past_key, got_past_value = passed_along((got_key, got_value), "stretch", 1)
    head_queries = got_query[0]
    total_tokens = got_key.shape[1]
    position = jnp.arange(total_tokens)
    later = lax.axis_index("stretch") > 0
    past_visible = jnp.logical_and(position >= cache_from[0], later)
    visible = jnp.concatenate([jnp.ones((total_tokens,), bool), past_visible])
    keys_all = jnp.concatenate([got_key[0], got_past_key[0]], 0)
    values_all = jnp.concatenate([got_value[0], got_past_value[0]], 0)
    span = math.gcd(512, 2 * total_tokens)
    count_blocks = 2 * total_tokens // span
    key_blocks = keys_all.reshape(count_blocks, span, per_dev, HD)
    value_blocks = values_all.reshape(count_blocks, span, per_dev, HD)
    visible_blocks = visible.reshape(count_blocks, span)
    query_count = head_queries.shape[0]
    scale = HD ** (-0.5)

    def absorb(carry, packed):
        largest, total, numer = carry
        key_block, value_block, seen = packed
        scores = (
            jnp.einsum("qhd,khd->hqk", head_queries, key_block, preferred_element_type=jnp.float32)
            * scale
        )
        scores = jnp.where(seen[None, None, :], scores, -1e30)
        updated = jnp.maximum(largest, jnp.max(scores, axis=2))
        factor = jnp.exp(largest - updated)
        weights = jnp.where(seen[None, None, :], jnp.exp(scores - updated[:, :, None]), 0.0)
        total = total * factor + jnp.sum(weights, axis=2)
        numer = numer * jnp.transpose(factor)[:, :, None] + jnp.einsum(
            "hqk,khd->qhd",
            weights.astype(jnp.bfloat16),
            value_block,
            preferred_element_type=jnp.float32,
        )
        return ((updated, total, numer), None)

    initial = (
        jnp.full((per_dev, query_count), -1e30, jnp.float32),
        jnp.zeros((per_dev, query_count), jnp.float32),
        jnp.zeros((query_count, per_dev, HD), jnp.float32),
    )
    (largest, total, numer), unused = lax.scan(
        absorb, initial, (key_blocks, value_blocks, visible_blocks)
    )
    attended = (numer / jnp.transpose(total)[:, :, None]).astype(jnp.bfloat16)
    returned = lax.all_to_all(attended[None], "seq", split_axis=1, concat_axis=0, tiled=True)
    tokens_out = returned.reshape(groups, blocks, part_len, per_dev, HD).transpose(1, 2, 0, 3, 4)
    tokens_out = tokens_out.reshape(own_count, HEADS * HD)
    matched = jnp.arange(gate_table.shape[0]) == time_index[0]
    gate_row = jnp.sum(jnp.where(matched[:, None], gate_table, 0.0), axis=0)
    attn_out = (tokens_out.astype(jnp.float32) * gate_row).astype(jnp.bfloat16)[None]
    return attn_out


def pack_kernel(query_ref, key_ref, value_ref, packed_ref):
    rows = query_ref.shape[0]
    for head in range(HEADS):
        lanes = pl.ds(head * HD, HD)
        for part, ref in enumerate((query_ref, key_ref, value_ref)):
            packed_ref[head, pl.ds(part * rows, rows), :] = ref[:, lanes]


def attend_kernel(cache_ref, time_ref, got_ref, gate_ref, out_ref, row_ref, sem):
    fetch = pltpu.make_async_copy(gate_ref.at[pl.ds(time_ref[0], 1)], row_ref, sem)
    fetch.start()
    clips = cache_ref.shape[0]
    devices, triple, _ = got_ref.shape
    seq, rows = devices // clips, triple // 3
    tokens = seq * rows

    def part(clip, which):
        block = got_ref[pl.ds(clip * seq, seq), pl.ds(which * rows, rows), :]
        return block.reshape(tokens, HD)

    def product(left, right, dims):
        return lax.dot_general(left, right, (dims, ((), ())), preferred_element_type=jnp.float32)

    scale = HD ** (-0.5)
    for clip in range(clips):
        query = part(clip, 0)
        own = product(query, part(clip, 1), ((1,), (1,))) * scale
        largest = jnp.max(own, axis=1, keepdims=True)
        if clip > 0:
            past = product(query, part(clip - 1, 1), ((1,), (1,))) * scale
            position = lax.broadcasted_iota(jnp.int32, past.shape, 1)
            past = jnp.where(position >= cache_ref[clip], past, -1e30)
            largest = jnp.maximum(largest, jnp.max(past, axis=1, keepdims=True))
        weights = jnp.exp(own - largest)
        total = jnp.sum(weights, axis=1, keepdims=True)
        numer = product(weights.astype(jnp.bfloat16), part(clip, 2), ((1,), (0,)))
        if clip > 0:
            weights = jnp.exp(past - largest)
            total += jnp.sum(weights, axis=1, keepdims=True)
            numer += product(weights.astype(jnp.bfloat16), part(clip - 1, 2), ((1,), (0,)))
        attended = (numer / total).astype(jnp.bfloat16)
        out_ref[pl.ds(clip * seq, seq)] = attended.reshape(seq, rows, HD)
    fetch.wait()


def unpack_kernel(got_ref, row_ref, out_ref):
    for head in range(HEADS):
        lanes = pl.ds(head * HD, HD)
        gated = got_ref[head].astype(jnp.float32) * row_ref[:, lanes]
        out_ref[:, lanes] = gated.astype(jnp.bfloat16)


def head_body(query_rows, key_rows, value_rows, cache_from, time_index, gate_table):
    axes = ("stretch", "seq")
    rows = query_rows.shape[1]
    clips = lax.axis_size("stretch")
    packed = pl.pallas_call(
        pack_kernel,
        out_shape=jax.ShapeDtypeStruct((HEADS, 3 * rows, HD), jnp.bfloat16),
        in_specs=[VMEM] * 3,
        out_specs=VMEM,
    )(query_rows[0], key_rows[0], value_rows[0])
    cache_all = lax.all_gather(cache_from, "stretch", tiled=True)
    got = lax.all_to_all(packed, axes, split_axis=0, concat_axis=0, tiled=True)
    attended, gate_row = pl.pallas_call(
        attend_kernel,
        out_shape=(
            jax.ShapeDtypeStruct((HEADS, rows, HD), jnp.bfloat16),
            jax.ShapeDtypeStruct((1, HEADS * HD), jnp.float32),
        ),
        in_specs=[SMEM, SMEM, VMEM, ANY],
        out_specs=(VMEM, VMEM),
        scratch_shapes=[pltpu.SemaphoreType.DMA],
    )(cache_all, time_index, got, gate_table)
    back = lax.all_to_all(attended, axes, split_axis=0, concat_axis=0, tiled=True)
    return pl.pallas_call(
        unpack_kernel,
        out_shape=jax.ShapeDtypeStruct((rows, HEADS * HD), jnp.bfloat16),
        in_specs=[VMEM, VMEM],
        out_specs=VMEM,
    )(back, gate_row)[None]


def solution(mesh):
    by_head = mesh.shape["stretch"] * mesh.shape["seq"] == HEADS
    return jax.shard_map(
        head_body if by_head else general_body,
        mesh=mesh,
        in_specs=(
            P("stretch", "seq", None),
            P("stretch", "seq", None),
            P("stretch", "seq", None),
            P("stretch"),
            P("stretch"),
            P(),
        ),
        out_specs=P("stretch", "seq", None),
        check_vma=False,
    )
```

```python
import math

import jax
import jax.numpy as jnp
from jax import lax
from jax.experimental import pallas as pl
from jax.experimental.pallas import tpu as pltpu
from jax.sharding import PartitionSpec as P

HEADS = 32
HD = 128
VMEM = pl.BlockSpec(memory_space=pltpu.VMEM)
SMEM = pl.BlockSpec(memory_space=pltpu.SMEM)
ANY = pl.BlockSpec(memory_space=pl.ANY)
HBM = pl.BlockSpec(memory_space=pltpu.HBM)


def passed_along(block, axis, distance):
    devices = range(lax.axis_size(axis))
    route = [(i - distance, i) for i in devices if i - distance in devices]
    return lax.ppermute(block, axis, route)


def spread(rows, groups, per_dev, blocks):
    count = rows.shape[0]
    arranged = rows.reshape(count, groups, per_dev, HD).transpose(1, 0, 2, 3)
    return jnp.repeat(arranged, blocks, axis=0)


def general_body(query_rows, key_rows, value_rows, cache_from, time_index, gate_table):
    seq_count = lax.axis_size("seq")
    own_count = query_rows.shape[1]
    blocks = max(seq_count // HEADS, 1)
    per_dev = HEADS * blocks // seq_count
    groups = HEADS // per_dev
    part_len = own_count // blocks
    queries = query_rows[0].reshape(blocks, part_len, groups, per_dev, HD).transpose(2, 0, 1, 3, 4)
    queries = queries.reshape(groups * blocks, part_len, per_dev, HD)
    got_query, got_key, got_value = (
        lax.all_to_all(queries, "seq", split_axis=0, concat_axis=1, tiled=True),
        lax.all_to_all(
            spread(key_rows[0], groups, per_dev, blocks),
            "seq",
            split_axis=0,
            concat_axis=1,
            tiled=True,
        ),
        lax.all_to_all(
            spread(value_rows[0], groups, per_dev, blocks),
            "seq",
            split_axis=0,
            concat_axis=1,
            tiled=True,
        ),
    )
    got_past_key, got_past_value = passed_along((got_key, got_value), "stretch", 1)
    head_queries = got_query[0]
    total_tokens = got_key.shape[1]
    position = jnp.arange(total_tokens)
    later = lax.axis_index("stretch") > 0
    past_visible = jnp.logical_and(position >= cache_from[0], later)
    visible = jnp.concatenate([jnp.ones((total_tokens,), bool), past_visible])
    keys_all = jnp.concatenate([got_key[0], got_past_key[0]], 0)
    values_all = jnp.concatenate([got_value[0], got_past_value[0]], 0)
    span = math.gcd(512, 2 * total_tokens)
    count_blocks = 2 * total_tokens // span
    key_blocks = keys_all.reshape(count_blocks, span, per_dev, HD)
    value_blocks = values_all.reshape(count_blocks, span, per_dev, HD)
    visible_blocks = visible.reshape(count_blocks, span)
    query_count = head_queries.shape[0]
    scale = HD ** (-0.5)

    def absorb(carry, packed):
        largest, total, numer = carry
        key_block, value_block, seen = packed
        scores = (
            jnp.einsum("qhd,khd->hqk", head_queries, key_block, preferred_element_type=jnp.float32)
            * scale
        )
        scores = jnp.where(seen[None, None, :], scores, -1e30)
        updated = jnp.maximum(largest, jnp.max(scores, axis=2))
        factor = jnp.exp(largest - updated)
        weights = jnp.where(seen[None, None, :], jnp.exp(scores - updated[:, :, None]), 0.0)
        total = total * factor + jnp.sum(weights, axis=2)
        numer = numer * jnp.transpose(factor)[:, :, None] + jnp.einsum(
            "hqk,khd->qhd",
            weights.astype(jnp.bfloat16),
            value_block,
            preferred_element_type=jnp.float32,
        )
        return ((updated, total, numer), None)

    initial = (
        jnp.full((per_dev, query_count), -1e30, jnp.float32),
        jnp.zeros((per_dev, query_count), jnp.float32),
        jnp.zeros((query_count, per_dev, HD), jnp.float32),
    )
    (largest, total, numer), unused = lax.scan(
        absorb, initial, (key_blocks, value_blocks, visible_blocks)
    )
    attended = (numer / jnp.transpose(total)[:, :, None]).astype(jnp.bfloat16)
    returned = lax.all_to_all(attended[None], "seq", split_axis=1, concat_axis=0, tiled=True)
    tokens_out = returned.reshape(groups, blocks, part_len, per_dev, HD).transpose(1, 2, 0, 3, 4)
    tokens_out = tokens_out.reshape(own_count, HEADS * HD)
    matched = jnp.arange(gate_table.shape[0]) == time_index[0]
    gate_row = jnp.sum(jnp.where(matched[:, None], gate_table, 0.0), axis=0)
    attn_out = (tokens_out.astype(jnp.float32) * gate_row).astype(jnp.bfloat16)[None]
    return attn_out


def chips_of(seq):
    return seq // 2


def steps_of(chips):
    return [step for step in range(1, chips) if step >= chips // 2] + list(range(1, chips // 2))


def span_of(chip, width):
    return pl.ds(pl.multiple_of(chip * width, width), width)


def pack_kernel(*refs):
    whole, parts, sems = refs[:3], refs[3:-1], refs[-1]
    chips = len(parts) // 3
    chip = lax.axis_index("seq") // 2
    copies = []
    for index, ref in enumerate(whole):
        width = ref.shape[1] // chips
        for place, step in enumerate([0] + steps_of(chips)):
            copies.append(
                pltpu.make_async_copy(
                    ref.at[:, span_of(chip ^ step, width)],
                    parts[index * chips + place],
                    sems.at[index * chips + place],
                )
            )
    for copy in copies:
        copy.start()
    for copy in copies:
        copy.wait()


def join_kernel(*refs):
    parts, out_ref = refs[:-1], refs[-1]
    rows = parts[0].shape[0]
    for place, part in enumerate(parts):
        out_ref[pl.ds(place * rows, rows)] = part[...]


def product(left, right, dims):
    return lax.dot_general(left, right, (dims, ((), ())), preferred_element_type=jnp.float32)


def weigh_kernel(cache_ref, *refs):
    chips = len(refs) - 9
    queries, refs = refs[:chips], refs[chips:]
    key_refs, value_refs, past_refs = refs[0:2], refs[2:4], refs[4:6]
    past_weight_ref, total_ref, numer_ref = refs[6:9]
    rows, width = queries[0].shape
    half = chips * rows
    tokens = 2 * half
    core = lax.rem(lax.axis_index("seq"), 2)
    chip = lax.axis_index("seq") // 2
    seen_from = jnp.where(lax.axis_index("stretch") > 0, cache_ref[0], tokens)
    steps = [0] + steps_of(chips)
    lane = lax.broadcasted_iota(jnp.int32, (1, rows), 1)
    position = jnp.concatenate(
        [
            lane + ((chip ^ step) * 2 + (core ^ other)) * rows
            for other in range(2)
            for step in steps
        ],
        axis=1,
    )
    visible = position >= seen_from
    scale = HD ** (-0.5)
    for head in range(width // HD):
        lanes = pl.ds(head * HD, HD)
        query = jnp.concatenate([ref[:, lanes] for ref in queries], axis=0)
        key = jnp.concatenate([ref[:, lanes] for ref in key_refs], axis=0)
        value = jnp.concatenate([ref[:, lanes] for ref in value_refs], axis=0)
        past_key = jnp.concatenate([ref[:, lanes] for ref in past_refs], axis=0)
        own = product(query, key, ((1,), (1,))) * scale
        past = product(query, past_key, ((1,), (1,))) * scale
        past = jnp.where(visible, past, -1e30)
        largest = jnp.max(jnp.maximum(own, past), axis=1, keepdims=True)
        own = jnp.exp(own - largest)
        past = jnp.exp(past - largest)
        total_ref[head] = jnp.sum(own + past, axis=1, keepdims=True)
        numer_ref[:, lanes] = product(own.astype(jnp.bfloat16), value, ((1,), (0,)))
        past_weight_ref[head] = past.astype(jnp.bfloat16)


def finish_kernel(time_ref, past_weight_ref, total_ref, numer_ref, *refs):
    past_refs, gate_ref = refs[0:2], refs[2]
    outs, gate_row, sem = refs[3:-2], refs[-2], refs[-1]
    chips = len(outs)
    width = outs[0].shape[1]
    rows = outs[0].shape[0]
    chip = lax.axis_index("seq") // 2
    fetch = pltpu.make_async_copy(gate_ref.at[pl.ds(time_ref[0], 1), span_of(chip, width)], gate_row, sem)
    fetch.start()
    fetch.wait()
    for head in range(width // HD):
        lanes = pl.ds(head * HD, HD)
        past_value = jnp.concatenate([ref[:, lanes] for ref in past_refs], axis=0)
        numer = numer_ref[:, lanes] + product(past_weight_ref[head], past_value, ((1,), (0,)))
        attended = (numer / total_ref[head]).astype(jnp.bfloat16)
        gated = (attended.astype(jnp.float32) * gate_row[:, lanes]).astype(jnp.bfloat16)
        for place in range(chips):
            outs[place][:, lanes] = gated[place * rows:(place + 1) * rows]


def unpack_kernel(*refs):
    parts, out_ref, sems = refs[:-2], refs[-2], refs[-1]
    chips = len(parts)
    chip = lax.axis_index("seq") // 2
    width = parts[0].shape[1]
    copies = [
        pltpu.make_async_copy(part, out_ref.at[:, span_of(chip ^ step, width)], sems.at[place])
        for place, (part, step) in enumerate(zip(parts, [0] + steps_of(chips)))
    ]
    for copy in copies:
        copy.start()
    for copy in copies:
        copy.wait()


def kernel_call(kernel, ins, outs, scratch=(), work=0):
    many = isinstance(outs, tuple)
    call = pl.pallas_call(
        kernel,
        out_shape=jax.tree.map(lambda out: pltpu.VMEM(out.shape, out.dtype), outs),
        in_specs=ins,
        out_specs=(VMEM,) * len(outs) if many else VMEM,
        scratch_shapes=[*scratch],
        cost_estimate=pl.CostEstimate(flops=work, bytes_accessed=0, transcendentals=0),
        compiler_params=pltpu.CompilerParams(vmem_limit_bytes=4 << 20),
    )

    def run(*operands):
        return call(
            *(
                pltpu.with_memory_space_constraint(operand, spec.memory_space)
                if spec in (VMEM, HBM)
                else operand
                for operand, spec in zip(operands, ins)
            )
        )

    return run


def chip_body(query_rows, key_rows, value_rows, cache_from, time_index, gate_table):
    seq = lax.axis_size("seq")
    chips = chips_of(seq)
    rows = query_rows.shape[1]
    width = HEADS * HD // chips
    half = chips * rows
    steps = steps_of(chips)
    block = jax.ShapeDtypeStruct((rows, width), jnp.bfloat16)
    joined = jax.ShapeDtypeStruct((half, width), jnp.bfloat16)

    def between_chips(parts):
        return [parts[0]] + [
            lax.ppermute(part, "seq", [(i, i ^ (2 * step)) for i in range(seq)])
            for part, step in zip(parts[1:], steps)
        ]

    def between_cores(part):
        return lax.ppermute(part, "seq", [(i, i ^ 1) for i in range(seq)])

    def join(parts):
        return kernel_call(join_kernel, [VMEM] * chips, joined)(*parts)

    parts = kernel_call(
        pack_kernel,
        [HBM] * 3,
        (block,) * (3 * chips),
        scratch=[pltpu.SemaphoreType.DMA((3 * chips,))],
    )(
        key_rows[0], value_rows[0], query_rows[0]
    )
    keys = join(between_chips(parts[:chips]))
    past_keys = passed_along(keys, "stretch", 1)
    values = join(between_chips(parts[chips:2 * chips]))
    past_values = passed_along(values, "stretch", 1)
    queries = between_chips(parts[2 * chips:])
    queries, keys, values = lax.optimization_barrier((queries, keys, values))
    per_dev = width // HD
    past_weight, total, numer = kernel_call(
        weigh_kernel,
        [SMEM] + [VMEM] * (chips + 6),
        (
            jax.ShapeDtypeStruct((per_dev, half, 2 * half), jnp.bfloat16),
            jax.ShapeDtypeStruct((per_dev, half, 1), jnp.float32),
            jax.ShapeDtypeStruct((half, width), jnp.float32),
        ),
    )(
        cache_from,
        *queries,
        keys,
        between_cores(keys),
        values,
        between_cores(values),
        past_keys,
        between_cores(past_keys),
    )
    outs = kernel_call(
        finish_kernel,
        [SMEM] + [VMEM] * 5 + [ANY],
        (block,) * chips,
        scratch=[pltpu.VMEM((1, width), jnp.float32), pltpu.SemaphoreType.DMA],
    )(time_index, past_weight, total, numer, past_values, between_cores(past_values), gate_table)
    returned = between_chips(outs)
    out = pl.pallas_call(
        unpack_kernel,
        out_shape=jax.ShapeDtypeStruct((rows, HEADS * HD), jnp.bfloat16),
        in_specs=[VMEM] * chips,
        out_specs=ANY,
        scratch_shapes=[pltpu.SemaphoreType.DMA((chips,))],
    )(*(pltpu.with_memory_space_constraint(part, pltpu.VMEM) for part in returned))
    return out[None]


def solution(mesh):
    chips = chips_of(mesh.shape["seq"])
    by_chip = HEADS % chips == 0 and chips & (chips - 1) == 0
    return jax.shard_map(
        chip_body if by_chip else general_body,
        mesh=mesh,
        in_specs=(
            P("stretch", "seq", None),
            P("stretch", "seq", None),
            P("stretch", "seq", None),
            P("stretch"),
            P("stretch"),
            P(),
        ),
        out_specs=P("stretch", "seq", None),
        check_vma=False,
    )
```

```python
import functools
import math

import jax
import jax.numpy as jnp
from jax import lax
from jax.experimental import pallas as pl
from jax.experimental.pallas import tpu as pltpu
from jax.sharding import PartitionSpec as P

HEADS = 32
HD = 128
VMEM = pl.BlockSpec(memory_space=pltpu.VMEM)
SMEM = pl.BlockSpec(memory_space=pltpu.SMEM)
ANY = pl.BlockSpec(memory_space=pl.ANY)
HBM = pl.BlockSpec(memory_space=pltpu.HBM)


def passed_along(block, axis, distance):
    devices = range(lax.axis_size(axis))
    route = [(i - distance, i) for i in devices if i - distance in devices]
    return lax.ppermute(block, axis, route)


def spread(rows, groups, per_dev, blocks):
    count = rows.shape[0]
    arranged = rows.reshape(count, groups, per_dev, HD).transpose(1, 0, 2, 3)
    return jnp.repeat(arranged, blocks, axis=0)


def general_body(query_rows, key_rows, value_rows, cache_from, time_index, gate_table):
    seq_count = lax.axis_size("seq")
    own_count = query_rows.shape[1]
    blocks = max(seq_count // HEADS, 1)
    per_dev = HEADS * blocks // seq_count
    groups = HEADS // per_dev
    part_len = own_count // blocks
    queries = query_rows[0].reshape(blocks, part_len, groups, per_dev, HD).transpose(2, 0, 1, 3, 4)
    queries = queries.reshape(groups * blocks, part_len, per_dev, HD)
    got_query, got_key, got_value = (
        lax.all_to_all(queries, "seq", split_axis=0, concat_axis=1, tiled=True),
        lax.all_to_all(
            spread(key_rows[0], groups, per_dev, blocks),
            "seq",
            split_axis=0,
            concat_axis=1,
            tiled=True,
        ),
        lax.all_to_all(
            spread(value_rows[0], groups, per_dev, blocks),
            "seq",
            split_axis=0,
            concat_axis=1,
            tiled=True,
        ),
    )
    got_past_key, got_past_value = passed_along((got_key, got_value), "stretch", 1)
    head_queries = got_query[0]
    total_tokens = got_key.shape[1]
    position = jnp.arange(total_tokens)
    later = lax.axis_index("stretch") > 0
    past_visible = jnp.logical_and(position >= cache_from[0], later)
    visible = jnp.concatenate([jnp.ones((total_tokens,), bool), past_visible])
    keys_all = jnp.concatenate([got_key[0], got_past_key[0]], 0)
    values_all = jnp.concatenate([got_value[0], got_past_value[0]], 0)
    span = math.gcd(512, 2 * total_tokens)
    count_blocks = 2 * total_tokens // span
    key_blocks = keys_all.reshape(count_blocks, span, per_dev, HD)
    value_blocks = values_all.reshape(count_blocks, span, per_dev, HD)
    visible_blocks = visible.reshape(count_blocks, span)
    query_count = head_queries.shape[0]
    scale = HD ** (-0.5)

    def absorb(carry, packed):
        largest, total, numer = carry
        key_block, value_block, seen = packed
        scores = (
            jnp.einsum("qhd,khd->hqk", head_queries, key_block, preferred_element_type=jnp.float32)
            * scale
        )
        scores = jnp.where(seen[None, None, :], scores, -1e30)
        updated = jnp.maximum(largest, jnp.max(scores, axis=2))
        factor = jnp.exp(largest - updated)
        weights = jnp.where(seen[None, None, :], jnp.exp(scores - updated[:, :, None]), 0.0)
        total = total * factor + jnp.sum(weights, axis=2)
        numer = numer * jnp.transpose(factor)[:, :, None] + jnp.einsum(
            "hqk,khd->qhd",
            weights.astype(jnp.bfloat16),
            value_block,
            preferred_element_type=jnp.float32,
        )
        return ((updated, total, numer), None)

    initial = (
        jnp.full((per_dev, query_count), -1e30, jnp.float32),
        jnp.zeros((per_dev, query_count), jnp.float32),
        jnp.zeros((query_count, per_dev, HD), jnp.float32),
    )
    (largest, total, numer), unused = lax.scan(
        absorb, initial, (key_blocks, value_blocks, visible_blocks)
    )
    attended = (numer / jnp.transpose(total)[:, :, None]).astype(jnp.bfloat16)
    returned = lax.all_to_all(attended[None], "seq", split_axis=1, concat_axis=0, tiled=True)
    tokens_out = returned.reshape(groups, blocks, part_len, per_dev, HD).transpose(1, 2, 0, 3, 4)
    tokens_out = tokens_out.reshape(own_count, HEADS * HD)
    matched = jnp.arange(gate_table.shape[0]) == time_index[0]
    gate_row = jnp.sum(jnp.where(matched[:, None], gate_table, 0.0), axis=0)
    attn_out = (tokens_out.astype(jnp.float32) * gate_row).astype(jnp.bfloat16)[None]
    return attn_out


CHIPS = 4
STEPS_IN = (3, 1, 2)
STEPS_OUT = (3, 2, 1)
QUERY_SHARES = ((2,), (1, 3))


def span_of(chip, width):
    return pl.ds(pl.multiple_of(chip * width, width), width)


def run_copies(copies):
    for copy in copies:
        copy.start()
    for copy in copies:
        copy.wait()


def pack_kernel(cuts, *refs):
    whole, parts, sems = refs[:3], refs[3:-1], refs[-1]
    rows = whole[0].shape[0]
    width = parts[0].shape[1]
    chip = lax.axis_index("seq") // 2
    copies = []
    for part, (index, steps) in zip(parts, cuts):
        for place, step in enumerate(steps):
            copies.append(
                pltpu.make_async_copy(
                    whole[index].at[:, span_of(chip ^ step, width)],
                    part.at[pl.ds(place * rows, rows)],
                    sems.at[len(copies)],
                )
            )
    run_copies(copies)


def join_kernel(places, *refs):
    parts, out_ref = refs[:-1], refs[-1]
    rows = out_ref.shape[0] // len(parts)
    for part, (to, place) in zip(parts, places):
        out_ref[pl.ds(to * rows, rows)] = part[pl.ds(place * rows, rows)]


def product(left, right, dims):
    return lax.dot_general(left, right, (dims, ((), ())), preferred_element_type=jnp.float32)


def weigh_kernel(cache_ref, *refs):
    queries, refs = refs[0], refs[1:]
    chips = CHIPS
    key_refs, value_refs, past_refs = refs[0:2], refs[2:4], refs[4:6]
    past_weight_ref, total_ref, numer_ref = refs[6:9]
    half, width = queries.shape
    rows = half // chips
    tokens = 2 * half
    core = lax.rem(lax.axis_index("seq"), 2)
    chip = lax.axis_index("seq") // 2
    seen_from = jnp.where(lax.axis_index("stretch") > 0, cache_ref[0], tokens)
    steps = range(chips)
    lane = lax.broadcasted_iota(jnp.int32, (1, rows), 1)
    position = jnp.concatenate(
        [
            lane + ((chip ^ step) * 2 + (core ^ other)) * rows
            for other in range(2)
            for step in steps
        ],
        axis=1,
    )
    visible = position >= seen_from
    scale = HD ** (-0.5) * math.log2(math.e)

    def scores(head):
        lanes = pl.ds(head * HD, HD)
        query = queries[:, lanes]
        key = jnp.concatenate([ref[:, lanes] for ref in key_refs], axis=0)
        value = jnp.concatenate([ref[:, lanes] for ref in value_refs], axis=0)
        past_key = jnp.concatenate([ref[:, lanes] for ref in past_refs], axis=0)
        own = product(query, key, ((1,), (1,)))
        past = product(query, past_key, ((1,), (1,)))
        return own, past, value

    def mix(head, own, value):
        numer_ref[:, pl.ds(head * HD, HD)] = product(own, value, ((1,), (0,)))

    heads = width // HD
    ready, weighed = scores(0), None
    for head in range(heads):
        own, past, value = ready
        if head + 1 < heads:
            ready = scores(head + 1)
        if weighed is not None:
            mix(*weighed)
        past = jnp.where(visible, past, -1e30)
        largest = jnp.max(jnp.maximum(own, past), axis=1, keepdims=True)
        own = jnp.exp2((own - largest) * scale)
        past = jnp.exp2((past - largest) * scale)
        total_ref[head] = jnp.sum(own + past, axis=1, keepdims=True)
        past_weight_ref[head] = past.astype(jnp.bfloat16)
        weighed = (head, own.astype(jnp.bfloat16), value)
    mix(*weighed)


def finish_kernel(time_ref, past_weight_ref, total_ref, numer_ref, *refs):
    past_refs, gate_ref = refs[0:2], refs[2]
    outs, gate_row, sem = refs[3:-2], refs[-2], refs[-1]
    chips = len(outs)
    width = outs[0].shape[1]
    rows = outs[0].shape[0]
    chip = lax.axis_index("seq") // 2
    fetch = pltpu.make_async_copy(gate_ref.at[pl.ds(time_ref[0], 1), span_of(chip, width)], gate_row, sem)
    fetch.start()
    fetch.wait()
    for head in range(width // HD):
        lanes = pl.ds(head * HD, HD)
        past_value = jnp.concatenate([ref[:, lanes] for ref in past_refs], axis=0)
        numer = numer_ref[:, lanes] + product(past_weight_ref[head], past_value, ((1,), (0,)))
        attended = (numer / total_ref[head]).astype(jnp.bfloat16)
        gated = (attended.astype(jnp.float32) * gate_row[:, lanes]).astype(jnp.bfloat16)
        for place in range(chips):
            outs[place][:, lanes] = gated[place * rows:(place + 1) * rows]


def unpack_kernel(*refs):
    parts, out_ref, sems = refs[:-2], refs[-2], refs[-1]
    chip = lax.axis_index("seq") // 2
    width = parts[0].shape[1]
    run_copies(
        [
            pltpu.make_async_copy(part, out_ref.at[:, span_of(chip ^ step, width)], sems.at[place])
            for place, (part, step) in enumerate(zip(parts, (0, *STEPS_OUT)))
        ]
    )


def kernel_call(kernel, ins, outs, scratch=(), work=0):
    many = isinstance(outs, tuple)
    call = pl.pallas_call(
        kernel,
        out_shape=jax.tree.map(lambda out: pltpu.VMEM(out.shape, out.dtype), outs),
        in_specs=ins,
        out_specs=(VMEM,) * len(outs) if many else VMEM,
        scratch_shapes=[*scratch],
        cost_estimate=pl.CostEstimate(flops=work, bytes_accessed=0, transcendentals=0),
        compiler_params=pltpu.CompilerParams(vmem_limit_bytes=4 << 20),
    )

    def run(*operands):
        return call(
            *(
                pltpu.with_memory_space_constraint(operand, spec.memory_space)
                if spec in (VMEM, HBM)
                else operand
                for operand, spec in zip(operands, ins)
            )
        )

    return run


def after(value, *others):
    return lax.optimization_barrier((value, others))[0]


def chip_body(query_rows, key_rows, value_rows, cache_from, time_index, gate_table):
    seq = lax.axis_size("seq")
    rows = query_rows.shape[1]
    width = HEADS * HD // CHIPS
    half = CHIPS * rows
    per_dev = width // HD

    def block(count):
        return jax.ShapeDtypeStruct((count * rows, width), jnp.bfloat16)

    def with_chip(part, step):
        return lax.ppermute(part, "seq", [(i, i ^ (2 * step)) for i in range(seq)])

    def with_core(part):
        return lax.ppermute(part, "seq", [(i, i ^ 1) for i in range(seq)])

    def join(parts, places, work=0):
        kernel = functools.partial(join_kernel, places)
        return kernel_call(kernel, [VMEM] * len(parts), block(len(parts)), work=work)(*parts)

    cuts = [(index, (step,)) for index in range(2) for step in (0, *STEPS_IN)]
    cuts += [(2, (0,))] + [(2, steps) for steps in QUERY_SHARES]
    parts = kernel_call(
        functools.partial(pack_kernel, cuts),
        [HBM] * 3,
        tuple(block(len(steps)) for _, steps in cuts),
        scratch=[pltpu.SemaphoreType.DMA((3 * CHIPS,))],
    )(key_rows[0], value_rows[0], query_rows[0])
    key_parts, value_parts, query_parts = parts[:CHIPS], parts[CHIPS:2 * CHIPS], parts[2 * CHIPS:]

    def gathered(parts, work=0):
        got = [parts[0]] + [with_chip(part, step) for part, step in zip(parts[1:], STEPS_IN)]
        return join(got, [(step, 0) for step in (0, *STEPS_IN)], work)

    keys = gathered(key_parts)
    values = gathered(value_parts)
    past_keys = passed_along(keys, "stretch", 1)
    past_values = passed_along(values, "stretch", 1)
    own_query, two_on, near = query_parts
    near = with_chip(near, 1)
    far = with_chip(join([after(two_on, values), near], [(0, 0), (1, 1)]), 2)
    queries = join([own_query, near, far, far], [(0, 0), (1, 0), (2, 0), (3, 1)])
    past_weight, total, numer = kernel_call(
        weigh_kernel,
        [SMEM] + [VMEM] * 7,
        (
            jax.ShapeDtypeStruct((per_dev, half, 2 * half), jnp.bfloat16),
            jax.ShapeDtypeStruct((per_dev, half, 1), jnp.float32),
            jax.ShapeDtypeStruct((half, width), jnp.float32),
        ),
    )(
        cache_from,
        queries,
        keys,
        with_core(keys),
        values,
        with_core(values),
        past_keys,
        with_core(after(past_keys, far)),
    )
    outs = kernel_call(
        finish_kernel,
        [SMEM] + [VMEM] * 5 + [ANY],
        (block(1),) * CHIPS,
        scratch=[pltpu.VMEM((1, width), jnp.float32), pltpu.SemaphoreType.DMA],
    )(
        time_index,
        past_weight,
        total,
        numer,
        past_values,
        with_core(after(past_values, far)),
        gate_table,
    )
    returned = [outs[0]] + [with_chip(outs[step], step) for step in STEPS_OUT]
    out = pl.pallas_call(
        unpack_kernel,
        out_shape=jax.ShapeDtypeStruct((rows, HEADS * HD), jnp.bfloat16),
        in_specs=[VMEM] * CHIPS,
        out_specs=ANY,
        scratch_shapes=[pltpu.SemaphoreType.DMA((CHIPS,))],
    )(*(pltpu.with_memory_space_constraint(part, pltpu.VMEM) for part in returned))
    return out[None]


def solution(mesh):
    by_chip = mesh.shape["seq"] == 2 * CHIPS
    return jax.shard_map(
        chip_body if by_chip else general_body,
        mesh=mesh,
        in_specs=(
            P("stretch", "seq", None),
            P("stretch", "seq", None),
            P("stretch", "seq", None),
            P("stretch"),
            P("stretch"),
            P(),
        ),
        out_specs=P("stretch", "seq", None),
        check_vma=False,
    )
```

```python
import functools
import math

import jax
import jax.numpy as jnp
from jax import lax
from jax.experimental import pallas as pl
from jax.experimental.pallas import tpu as pltpu
from jax.sharding import PartitionSpec as P

HEADS = 32
HD = 128
VMEM = pl.BlockSpec(memory_space=pltpu.VMEM)
SMEM = pl.BlockSpec(memory_space=pltpu.SMEM)
ANY = pl.BlockSpec(memory_space=pl.ANY)
HBM = pl.BlockSpec(memory_space=pltpu.HBM)


def passed_along(block, axis, distance):
    devices = range(lax.axis_size(axis))
    route = [(i - distance, i) for i in devices if i - distance in devices]
    return lax.ppermute(block, axis, route)


def spread(rows, groups, per_dev, blocks):
    count = rows.shape[0]
    arranged = rows.reshape(count, groups, per_dev, HD).transpose(1, 0, 2, 3)
    return jnp.repeat(arranged, blocks, axis=0)


def general_body(query_rows, key_rows, value_rows, cache_from, time_index, gate_table):
    seq_count = lax.axis_size("seq")
    own_count = query_rows.shape[1]
    blocks = max(seq_count // HEADS, 1)
    per_dev = HEADS * blocks // seq_count
    groups = HEADS // per_dev
    part_len = own_count // blocks
    queries = query_rows[0].reshape(blocks, part_len, groups, per_dev, HD).transpose(2, 0, 1, 3, 4)
    queries = queries.reshape(groups * blocks, part_len, per_dev, HD)
    got_query, got_key, got_value = (
        lax.all_to_all(queries, "seq", split_axis=0, concat_axis=1, tiled=True),
        lax.all_to_all(
            spread(key_rows[0], groups, per_dev, blocks),
            "seq",
            split_axis=0,
            concat_axis=1,
            tiled=True,
        ),
        lax.all_to_all(
            spread(value_rows[0], groups, per_dev, blocks),
            "seq",
            split_axis=0,
            concat_axis=1,
            tiled=True,
        ),
    )
    got_past_key, got_past_value = passed_along((got_key, got_value), "stretch", 1)
    head_queries = got_query[0]
    total_tokens = got_key.shape[1]
    position = jnp.arange(total_tokens)
    later = lax.axis_index("stretch") > 0
    past_visible = jnp.logical_and(position >= cache_from[0], later)
    visible = jnp.concatenate([jnp.ones((total_tokens,), bool), past_visible])
    keys_all = jnp.concatenate([got_key[0], got_past_key[0]], 0)
    values_all = jnp.concatenate([got_value[0], got_past_value[0]], 0)
    span = math.gcd(512, 2 * total_tokens)
    count_blocks = 2 * total_tokens // span
    key_blocks = keys_all.reshape(count_blocks, span, per_dev, HD)
    value_blocks = values_all.reshape(count_blocks, span, per_dev, HD)
    visible_blocks = visible.reshape(count_blocks, span)
    query_count = head_queries.shape[0]
    scale = HD ** (-0.5)

    def absorb(carry, packed):
        largest, total, numer = carry
        key_block, value_block, seen = packed
        scores = (
            jnp.einsum("qhd,khd->hqk", head_queries, key_block, preferred_element_type=jnp.float32)
            * scale
        )
        scores = jnp.where(seen[None, None, :], scores, -1e30)
        updated = jnp.maximum(largest, jnp.max(scores, axis=2))
        factor = jnp.exp(largest - updated)
        weights = jnp.where(seen[None, None, :], jnp.exp(scores - updated[:, :, None]), 0.0)
        total = total * factor + jnp.sum(weights, axis=2)
        numer = numer * jnp.transpose(factor)[:, :, None] + jnp.einsum(
            "hqk,khd->qhd",
            weights.astype(jnp.bfloat16),
            value_block,
            preferred_element_type=jnp.float32,
        )
        return ((updated, total, numer), None)

    initial = (
        jnp.full((per_dev, query_count), -1e30, jnp.float32),
        jnp.zeros((per_dev, query_count), jnp.float32),
        jnp.zeros((query_count, per_dev, HD), jnp.float32),
    )
    (largest, total, numer), unused = lax.scan(
        absorb, initial, (key_blocks, value_blocks, visible_blocks)
    )
    attended = (numer / jnp.transpose(total)[:, :, None]).astype(jnp.bfloat16)
    returned = lax.all_to_all(attended[None], "seq", split_axis=1, concat_axis=0, tiled=True)
    tokens_out = returned.reshape(groups, blocks, part_len, per_dev, HD).transpose(1, 2, 0, 3, 4)
    tokens_out = tokens_out.reshape(own_count, HEADS * HD)
    matched = jnp.arange(gate_table.shape[0]) == time_index[0]
    gate_row = jnp.sum(jnp.where(matched[:, None], gate_table, 0.0), axis=0)
    attn_out = (tokens_out.astype(jnp.float32) * gate_row).astype(jnp.bfloat16)[None]
    return attn_out


CHIPS = 4


def following(chip):
    return 2 * (chip & 1) + 1 - (chip >> 1)


def preceding(chip):
    return 2 - 2 * (chip & 1) + (chip >> 1)


def facing(chip):
    return CHIPS - 1 - chip


ROUTES = ((following, preceding), (facing, facing), (preceding, following))
OUT_ORDER = (0, 1, 2)
KEY_ORDER = (1, 0, 2)
VALUE_ORDER = (0, 1, 2)


def span_of(chip, width):
    return pl.ds(pl.multiple_of(chip * width, width), width)


def run_copies(copies):
    for copy in copies:
        copy.start()
    for copy in copies:
        copy.wait()


def pack_kernel(cuts, *refs):
    whole, parts, sems = refs[:3], refs[3:-1], refs[-1]
    rows = whole[0].shape[0]
    width = parts[0].shape[1]
    here = lax.axis_index("seq") // 2
    copies = []
    for part, (index, chips) in zip(parts, cuts):
        for place, chip in enumerate(chips):
            copies.append(
                pltpu.make_async_copy(
                    whole[index].at[:, span_of(chip(here), width)],
                    part.at[pl.ds(place * rows, rows)],
                    sems.at[len(copies)],
                )
            )
    run_copies(copies)


def join_kernel(places, *refs):
    parts, out_ref = refs[:-1], refs[-1]
    rows = out_ref.shape[0] // len(parts)
    for part, (to, place) in zip(parts, places):
        out_ref[pl.ds(to * rows, rows)] = part[pl.ds(place * rows, rows)]


def query_kernel(own_ref, near_ref, far_ref, out_ref):
    rows = own_ref.shape[0]
    chip = lax.axis_index("seq") // 2
    near_place = jnp.where((chip ^ 1) == following(chip), 1, 3)
    out_ref[pl.ds(0, rows)] = own_ref[...]
    out_ref[pl.ds(2 * rows, rows)] = far_ref[pl.ds(rows, rows)]
    out_ref[pl.ds(pl.multiple_of(near_place * rows, rows), rows)] = near_ref[pl.ds(0, rows)]
    out_ref[pl.ds(pl.multiple_of((4 - near_place) * rows, rows), rows)] = far_ref[pl.ds(0, rows)]


def product(left, right, dims):
    return lax.dot_general(left, right, (dims, ((), ())), preferred_element_type=jnp.float32)


def weigh_kernel(cache_ref, *refs):
    queries, refs = refs[0], refs[1:]
    chips = CHIPS
    key_refs, value_refs, past_refs = refs[0:2], refs[2:4], refs[4:6]
    past_weight_ref, total_ref, numer_ref = refs[6:9]
    half, width = queries.shape
    rows = half // chips
    tokens = 2 * half
    core = lax.rem(lax.axis_index("seq"), 2)
    chip = lax.axis_index("seq") // 2
    seen_from = jnp.where(lax.axis_index("stretch") > 0, cache_ref[0], tokens)
    sources = [chip] + [source(chip) for _, source in ROUTES]
    lane = lax.broadcasted_iota(jnp.int32, (1, rows), 1)
    position = jnp.concatenate(
        [
            lane + (source * 2 + (core ^ other)) * rows
            for other in range(2)
            for source in sources
        ],
        axis=1,
    )
    visible = position >= seen_from
    scale = HD ** (-0.5) * math.log2(math.e)

    def scores(head):
        lanes = pl.ds(head * HD, HD)
        query = queries[:, lanes]
        key = jnp.concatenate([ref[:, lanes] for ref in key_refs], axis=0)
        value = jnp.concatenate([ref[:, lanes] for ref in value_refs], axis=0)
        past_key = jnp.concatenate([ref[:, lanes] for ref in past_refs], axis=0)
        own = product(query, key, ((1,), (1,)))
        past = product(query, past_key, ((1,), (1,)))
        return own, past, value

    def mix(head, own, value):
        numer_ref[:, pl.ds(head * HD, HD)] = product(own, value, ((1,), (0,)))

    heads = width // HD
    ready, weighed = scores(0), None
    for head in range(heads):
        own, past, value = ready
        if head + 1 < heads:
            ready = scores(head + 1)
        if weighed is not None:
            mix(*weighed)
        past = jnp.where(visible, past, -1e30)
        largest = jnp.max(jnp.maximum(own, past), axis=1, keepdims=True)
        own = jnp.exp2((own - largest) * scale)
        past = jnp.exp2((past - largest) * scale)
        total_ref[head] = jnp.sum(own + past, axis=1, keepdims=True)
        past_weight_ref[head] = past.astype(jnp.bfloat16)
        weighed = (head, own.astype(jnp.bfloat16), value)
    mix(*weighed)


def finish_kernel(time_ref, past_weight_ref, total_ref, numer_ref, *refs):
    past_refs, gate_ref = refs[0:2], refs[2]
    outs, gate_row, sem = refs[3:-2], refs[-2], refs[-1]
    chips = len(outs)
    width = outs[0].shape[1]
    rows = outs[0].shape[0]
    chip = lax.axis_index("seq") // 2
    fetch = pltpu.make_async_copy(gate_ref.at[pl.ds(time_ref[0], 1), span_of(chip, width)], gate_row, sem)
    fetch.start()
    fetch.wait()
    for head in range(width // HD):
        lanes = pl.ds(head * HD, HD)
        past_value = jnp.concatenate([ref[:, lanes] for ref in past_refs], axis=0)
        numer = numer_ref[:, lanes] + product(past_weight_ref[head], past_value, ((1,), (0,)))
        attended = (numer / total_ref[head]).astype(jnp.bfloat16)
        gated = (attended.astype(jnp.float32) * gate_row[:, lanes]).astype(jnp.bfloat16)
        for place in range(chips):
            outs[place][:, lanes] = gated[place * rows:(place + 1) * rows]


def unpack_kernel(*refs):
    parts, out_ref, sems = refs[:-2], refs[-2], refs[-1]
    chip = lax.axis_index("seq") // 2
    width = parts[0].shape[1]
    sources = [chip] + [ROUTES[route][1](chip) for route in OUT_ORDER]
    run_copies(
        [
            pltpu.make_async_copy(part, out_ref.at[:, span_of(source, width)], sems.at[place])
            for place, (part, source) in enumerate(zip(parts, sources))
        ]
    )


def kernel_call(kernel, ins, outs, scratch=(), work=0):
    many = isinstance(outs, tuple)
    call = pl.pallas_call(
        kernel,
        out_shape=jax.tree.map(lambda out: pltpu.VMEM(out.shape, out.dtype), outs),
        in_specs=ins,
        out_specs=(VMEM,) * len(outs) if many else VMEM,
        scratch_shapes=[*scratch],
        cost_estimate=pl.CostEstimate(flops=work, bytes_accessed=0, transcendentals=0),
        compiler_params=pltpu.CompilerParams(vmem_limit_bytes=4 << 20),
    )

    def run(*operands):
        return call(
            *(
                pltpu.with_memory_space_constraint(operand, spec.memory_space)
                if spec in (VMEM, HBM)
                else operand
                for operand, spec in zip(operands, ins)
            )
        )

    return run


def after(value, *others):
    return lax.optimization_barrier((value, others))[0]


def chip_body(query_rows, key_rows, value_rows, cache_from, time_index, gate_table):
    seq = lax.axis_size("seq")
    rows = query_rows.shape[1]
    width = HEADS * HD // CHIPS
    half = CHIPS * rows
    per_dev = width // HD

    def block(count):
        return jax.ShapeDtypeStruct((count * rows, width), jnp.bfloat16)

    def to_chip(part, target):
        return lax.ppermute(part, "seq", [(i, 2 * target(i // 2) + i % 2) for i in range(seq)])

    def with_core(part):
        return lax.ppermute(part, "seq", [(i, i ^ 1) for i in range(seq)])

    def join(parts, places, work=0):
        kernel = functools.partial(join_kernel, places)
        return kernel_call(kernel, [VMEM] * len(parts), block(len(parts)), work=work)(*parts)

    def stay(chip):
        return chip

    def away(step):
        return lambda chip: chip ^ step

    cuts = [(index, (chip,)) for index in range(2) for chip in (stay, *(to for to, _ in ROUTES))]
    cuts += [(2, (stay,)), (2, (away(2),)), (2, (away(1), away(3)))]
    parts = kernel_call(
        functools.partial(pack_kernel, cuts),
        [HBM] * 3,
        tuple(block(len(chips)) for _, chips in cuts),
        scratch=[pltpu.SemaphoreType.DMA((3 * CHIPS,))],
    )(key_rows[0], value_rows[0], query_rows[0])
    key_parts, value_parts, query_parts = parts[:CHIPS], parts[CHIPS:2 * CHIPS], parts[2 * CHIPS:]

    def gathered(parts, order, work=0):
        got = [parts[0]] + [to_chip(parts[1 + route], ROUTES[route][0]) for route in order]
        return join(got, [(0, 0)] + [(1 + route, 0) for route in order], work)

    keys = gathered(key_parts, KEY_ORDER)
    values = gathered(value_parts, VALUE_ORDER)
    past_keys = passed_along(keys, "stretch", 1)
    past_values = passed_along(values, "stretch", 1)
    own_query, two_on, near = query_parts
    near = to_chip(near, away(1))
    far = to_chip(join([after(two_on, values), near], [(0, 0), (1, 1)]), away(2))
    queries = kernel_call(query_kernel, [VMEM] * 3, block(CHIPS))(own_query, near, far)
    past_weight, total, numer = kernel_call(
        weigh_kernel,
        [SMEM] + [VMEM] * 7,
        (
            jax.ShapeDtypeStruct((per_dev, half, 2 * half), jnp.bfloat16),
            jax.ShapeDtypeStruct((per_dev, half, 1), jnp.float32),
            jax.ShapeDtypeStruct((half, width), jnp.float32),
        ),
    )(
        cache_from,
        queries,
        keys,
        with_core(keys),
        values,
        with_core(values),
        past_keys,
        with_core(after(past_keys, far)),
    )
    outs = kernel_call(
        finish_kernel,
        [SMEM] + [VMEM] * 5 + [ANY],
        (block(1),) * CHIPS,
        scratch=[pltpu.VMEM((1, width), jnp.float32), pltpu.SemaphoreType.DMA],
    )(
        time_index,
        past_weight,
        total,
        numer,
        past_values,
        with_core(after(past_values, far)),
        gate_table,
    )
    returned = [outs[0]] + [to_chip(outs[1 + route], ROUTES[route][0]) for route in OUT_ORDER]
    out = pl.pallas_call(
        unpack_kernel,
        out_shape=jax.ShapeDtypeStruct((rows, HEADS * HD), jnp.bfloat16),
        in_specs=[VMEM] * CHIPS,
        out_specs=ANY,
        scratch_shapes=[pltpu.SemaphoreType.DMA((CHIPS,))],
    )(*(pltpu.with_memory_space_constraint(part, pltpu.VMEM) for part in returned))
    return out[None]


def solution(mesh):
    by_chip = mesh.shape["seq"] == 2 * CHIPS
    return jax.shard_map(
        chip_body if by_chip else general_body,
        mesh=mesh,
        in_specs=(
            P("stretch", "seq", None),
            P("stretch", "seq", None),
            P("stretch", "seq", None),
            P("stretch"),
            P("stretch"),
            P(),
        ),
        out_specs=P("stretch", "seq", None),
        check_vma=False,
    )
```

```python
import functools
import math

import jax
import jax.numpy as jnp
from jax import lax
from jax.experimental import pallas as pl
from jax.experimental.pallas import tpu as pltpu
from jax.sharding import PartitionSpec as P

HEADS = 32
HD = 128
VMEM = pl.BlockSpec(memory_space=pltpu.VMEM)
SMEM = pl.BlockSpec(memory_space=pltpu.SMEM)
ANY = pl.BlockSpec(memory_space=pl.ANY)
HBM = pl.BlockSpec(memory_space=pltpu.HBM)


def passed_along(block, axis, distance):
    devices = range(lax.axis_size(axis))
    route = [(i - distance, i) for i in devices if i - distance in devices]
    return lax.ppermute(block, axis, route)


def spread(rows, groups, per_dev, blocks):
    count = rows.shape[0]
    arranged = rows.reshape(count, groups, per_dev, HD).transpose(1, 0, 2, 3)
    return jnp.repeat(arranged, blocks, axis=0)


def general_body(query_rows, key_rows, value_rows, cache_from, time_index, gate_table):
    seq_count = lax.axis_size("seq")
    own_count = query_rows.shape[1]
    blocks = max(seq_count // HEADS, 1)
    per_dev = HEADS * blocks // seq_count
    groups = HEADS // per_dev
    part_len = own_count // blocks
    queries = query_rows[0].reshape(blocks, part_len, groups, per_dev, HD).transpose(2, 0, 1, 3, 4)
    queries = queries.reshape(groups * blocks, part_len, per_dev, HD)
    got_query, got_key, got_value = (
        lax.all_to_all(queries, "seq", split_axis=0, concat_axis=1, tiled=True),
        lax.all_to_all(
            spread(key_rows[0], groups, per_dev, blocks),
            "seq",
            split_axis=0,
            concat_axis=1,
            tiled=True,
        ),
        lax.all_to_all(
            spread(value_rows[0], groups, per_dev, blocks),
            "seq",
            split_axis=0,
            concat_axis=1,
            tiled=True,
        ),
    )
    got_past_key, got_past_value = passed_along((got_key, got_value), "stretch", 1)
    head_queries = got_query[0]
    total_tokens = got_key.shape[1]
    position = jnp.arange(total_tokens)
    later = lax.axis_index("stretch") > 0
    past_visible = jnp.logical_and(position >= cache_from[0], later)
    visible = jnp.concatenate([jnp.ones((total_tokens,), bool), past_visible])
    keys_all = jnp.concatenate([got_key[0], got_past_key[0]], 0)
    values_all = jnp.concatenate([got_value[0], got_past_value[0]], 0)
    span = math.gcd(512, 2 * total_tokens)
    count_blocks = 2 * total_tokens // span
    key_blocks = keys_all.reshape(count_blocks, span, per_dev, HD)
    value_blocks = values_all.reshape(count_blocks, span, per_dev, HD)
    visible_blocks = visible.reshape(count_blocks, span)
    query_count = head_queries.shape[0]
    scale = HD ** (-0.5)

    def absorb(carry, packed):
        largest, total, numer = carry
        key_block, value_block, seen = packed
        scores = (
            jnp.einsum("qhd,khd->hqk", head_queries, key_block, preferred_element_type=jnp.float32)
            * scale
        )
        scores = jnp.where(seen[None, None, :], scores, -1e30)
        updated = jnp.maximum(largest, jnp.max(scores, axis=2))
        factor = jnp.exp(largest - updated)
        weights = jnp.where(seen[None, None, :], jnp.exp(scores - updated[:, :, None]), 0.0)
        total = total * factor + jnp.sum(weights, axis=2)
        numer = numer * jnp.transpose(factor)[:, :, None] + jnp.einsum(
            "hqk,khd->qhd",
            weights.astype(jnp.bfloat16),
            value_block,
            preferred_element_type=jnp.float32,
        )
        return ((updated, total, numer), None)

    initial = (
        jnp.full((per_dev, query_count), -1e30, jnp.float32),
        jnp.zeros((per_dev, query_count), jnp.float32),
        jnp.zeros((query_count, per_dev, HD), jnp.float32),
    )
    (largest, total, numer), unused = lax.scan(
        absorb, initial, (key_blocks, value_blocks, visible_blocks)
    )
    attended = (numer / jnp.transpose(total)[:, :, None]).astype(jnp.bfloat16)
    returned = lax.all_to_all(attended[None], "seq", split_axis=1, concat_axis=0, tiled=True)
    tokens_out = returned.reshape(groups, blocks, part_len, per_dev, HD).transpose(1, 2, 0, 3, 4)
    tokens_out = tokens_out.reshape(own_count, HEADS * HD)
    matched = jnp.arange(gate_table.shape[0]) == time_index[0]
    gate_row = jnp.sum(jnp.where(matched[:, None], gate_table, 0.0), axis=0)
    attn_out = (tokens_out.astype(jnp.float32) * gate_row).astype(jnp.bfloat16)[None]
    return attn_out


CHIPS = 4


def following(chip):
    return 2 * (chip & 1) + 1 - (chip >> 1)


def preceding(chip):
    return 2 - 2 * (chip & 1) + (chip >> 1)


def facing(chip):
    return CHIPS - 1 - chip


ROUTES = ((following, preceding), (facing, facing), (preceding, following))
OUT_ORDER = (0, 1, 2)
KEY_ORDER = (1, 0, 2)
VALUE_ORDER = (0, 1, 2)


def span_of(chip, width):
    return pl.ds(pl.multiple_of(chip * width, width), width)


def run_copies(copies):
    for copy in copies:
        copy.start()
    for copy in copies:
        copy.wait()


def pack_kernel(cuts, *refs):
    whole, parts, sems = refs[:3], refs[3:-1], refs[-1]
    rows = whole[0].shape[0]
    width = parts[0].shape[1]
    here = lax.axis_index("seq") // 2
    copies = []
    for part, (index, chips) in zip(parts, cuts):
        for place, chip in enumerate(chips):
            copies.append(
                pltpu.make_async_copy(
                    whole[index].at[:, span_of(chip(here), width)],
                    part.at[pl.ds(place * rows, rows)],
                    sems.at[len(copies)],
                )
            )
    run_copies(copies)


def join_kernel(places, *refs):
    parts, out_ref = refs[:-1], refs[-1]
    rows = out_ref.shape[0] // len(parts)
    for part, (to, place) in zip(parts, places):
        out_ref[pl.ds(to * rows, rows)] = part[pl.ds(place * rows, rows)]


def query_kernel(own_ref, near_ref, far_ref, out_ref):
    rows = own_ref.shape[0]
    chip = lax.axis_index("seq") // 2
    near_place = jnp.where((chip ^ 1) == following(chip), 1, 3)
    out_ref[pl.ds(0, rows)] = own_ref[...]
    out_ref[pl.ds(2 * rows, rows)] = far_ref[pl.ds(rows, rows)]
    out_ref[pl.ds(pl.multiple_of(near_place * rows, rows), rows)] = near_ref[pl.ds(0, rows)]
    out_ref[pl.ds(pl.multiple_of((4 - near_place) * rows, rows), rows)] = far_ref[pl.ds(0, rows)]


def product(left, right, dims):
    return lax.dot_general(left, right, (dims, ((), ())), preferred_element_type=jnp.float32)


def prepare_kernel(cache_ref, time_ref, gate_ref, from_ref, row_ref, sem):
    chip = lax.axis_index("seq") // 2
    copy = pltpu.make_async_copy(
        gate_ref.at[pl.ds(time_ref[0], 1), span_of(chip, row_ref.shape[1])], row_ref, sem
    )
    copy.start()
    tokens = from_ref.shape[1]
    seen_from = jnp.where(lax.axis_index("stretch") > 0, cache_ref[0], tokens)
    from_ref[...] = jnp.full(from_ref.shape, seen_from, jnp.int32)
    copy.wait()


def weigh_kernel(from_ref, *refs):
    queries, refs = refs[0], refs[1:]
    chips = CHIPS
    key_refs, value_refs, past_refs = refs[0:2], refs[2:4], refs[4:6]
    past_weight_ref, total_ref, numer_ref = refs[6:9]
    half, width = queries.shape
    rows = half // chips
    core = lax.rem(lax.axis_index("seq"), 2)
    chip = lax.axis_index("seq") // 2
    sources = [chip] + [source(chip) for _, source in ROUTES]
    lane = lax.broadcasted_iota(jnp.int32, (1, rows), 1)
    position = jnp.concatenate(
        [
            lane + (source * 2 + (core ^ other)) * rows
            for other in range(2)
            for source in sources
        ],
        axis=1,
    )
    visible = position >= from_ref[...]
    scale = HD ** (-0.5) * math.log2(math.e)

    def scores(head):
        lanes = pl.ds(head * HD, HD)
        query = queries[:, lanes]
        key = jnp.concatenate([ref[:, lanes] for ref in key_refs], axis=0)
        value = jnp.concatenate([ref[:, lanes] for ref in value_refs], axis=0)
        past_key = jnp.concatenate([ref[:, lanes] for ref in past_refs], axis=0)
        own = product(query, key, ((1,), (1,)))
        past = product(query, past_key, ((1,), (1,)))
        return own, past, value

    def mix(head, own, value):
        numer_ref[:, pl.ds(head * HD, HD)] = product(own, value, ((1,), (0,)))

    heads = width // HD
    ready, weighed = scores(0), None
    for head in range(heads):
        own, past, value = ready
        if head + 1 < heads:
            ready = scores(head + 1)
        if weighed is not None:
            mix(*weighed)
        past = jnp.where(visible, past, -1e30)
        largest = jnp.max(jnp.maximum(own, past), axis=1, keepdims=True)
        own = jnp.exp2((own - largest) * scale)
        past = jnp.exp2((past - largest) * scale)
        total_ref[head] = jnp.sum(own + past, axis=1, keepdims=True)
        past_weight_ref[head] = past.astype(jnp.bfloat16)
        weighed = (head, own.astype(jnp.bfloat16), value)
    mix(*weighed)


def finish_kernel(past_weight_ref, total_ref, numer_ref, gate_row, *refs):
    past_refs, outs = refs[:2], refs[2:]
    rows, width = outs[0].shape
    for head in range(width // HD):
        lanes = pl.ds(head * HD, HD)
        past_value = jnp.concatenate([ref[:, lanes] for ref in past_refs], axis=0)
        numer = numer_ref[:, lanes] + product(past_weight_ref[head], past_value, ((1,), (0,)))
        attended = (numer / total_ref[head]).astype(jnp.bfloat16)
        gated = (attended.astype(jnp.float32) * gate_row[:, lanes]).astype(jnp.bfloat16)
        for place in range(CHIPS):
            outs[place][:, lanes] = gated[place * rows:(place + 1) * rows]


def unpack_kernel(*refs):
    parts, out_ref, sems = refs[:-2], refs[-2], refs[-1]
    chip = lax.axis_index("seq") // 2
    width = parts[0].shape[1]
    sources = [chip] + [ROUTES[route][1](chip) for route in OUT_ORDER]
    run_copies(
        [
            pltpu.make_async_copy(part, out_ref.at[:, span_of(source, width)], sems.at[place])
            for place, (part, source) in enumerate(zip(parts, sources))
        ]
    )


def kernel_call(kernel, ins, outs, scratch=(), work=0):
    many = isinstance(outs, tuple)
    call = pl.pallas_call(
        kernel,
        out_shape=jax.tree.map(lambda out: pltpu.VMEM(out.shape, out.dtype), outs),
        in_specs=ins,
        out_specs=(VMEM,) * len(outs) if many else VMEM,
        scratch_shapes=[*scratch],
        cost_estimate=pl.CostEstimate(flops=work, bytes_accessed=0, transcendentals=0),
        compiler_params=pltpu.CompilerParams(vmem_limit_bytes=4 << 20),
    )

    def run(*operands):
        return call(
            *(
                pltpu.with_memory_space_constraint(operand, spec.memory_space)
                if spec in (VMEM, HBM)
                else operand
                for operand, spec in zip(operands, ins)
            )
        )

    return run


def after(value, *others):
    return lax.optimization_barrier((value, others))[0]


def chip_body(query_rows, key_rows, value_rows, cache_from, time_index, gate_table):
    seq = lax.axis_size("seq")
    rows = query_rows.shape[1]
    width = HEADS * HD // CHIPS
    half = CHIPS * rows
    per_dev = width // HD

    def block(count):
        return jax.ShapeDtypeStruct((count * rows, width), jnp.bfloat16)

    def to_chip(part, target):
        return lax.ppermute(part, "seq", [(i, 2 * target(i // 2) + i % 2) for i in range(seq)])

    def with_core(part):
        return lax.ppermute(part, "seq", [(i, i ^ 1) for i in range(seq)])

    def join(parts, places, work=0):
        kernel = functools.partial(join_kernel, places)
        return kernel_call(kernel, [VMEM] * len(parts), block(len(parts)), work=work)(*parts)

    def stay(chip):
        return chip

    def away(step):
        return lambda chip: chip ^ step

    cuts = [(index, (chip,)) for index in range(2) for chip in (stay, *(to for to, _ in ROUTES))]
    cuts += [(2, (stay,)), (2, (away(2),)), (2, (away(1), away(3)))]
    parts = kernel_call(
        functools.partial(pack_kernel, cuts),
        [HBM] * 3,
        tuple(block(len(chips)) for _, chips in cuts),
        scratch=[pltpu.SemaphoreType.DMA((3 * CHIPS,))],
    )(key_rows[0], value_rows[0], query_rows[0])
    key_parts, value_parts, query_parts = parts[:CHIPS], parts[CHIPS:2 * CHIPS], parts[2 * CHIPS:]

    def gathered(parts, order, work=0):
        got = [parts[0]] + [to_chip(parts[1 + route], ROUTES[route][0]) for route in order]
        return join(got, [(0, 0)] + [(1 + route, 0) for route in order], work)

    keys = gathered(key_parts, KEY_ORDER)
    values = gathered(value_parts, VALUE_ORDER)
    past_keys = passed_along(keys, "stretch", 1)
    past_values = passed_along(values, "stretch", 1)
    own_query, two_on, near = query_parts
    near = to_chip(near, away(1))
    far = to_chip(join([after(two_on, values), near], [(0, 0), (1, 1)]), away(2))
    past_keys_too = with_core(past_keys)
    queries = kernel_call(query_kernel, [VMEM] * 3, block(CHIPS))(
        after(own_query, past_keys_too), near, far
    )
    seen_from, gate_row = kernel_call(
        prepare_kernel,
        [SMEM, SMEM, HBM],
        (
            jax.ShapeDtypeStruct((1, 2 * half), jnp.int32),
            jax.ShapeDtypeStruct((1, width), jnp.float32),
        ),
        scratch=[pltpu.SemaphoreType.DMA],
    )(cache_from, time_index, gate_table)
    past_weight, total, numer = kernel_call(
        weigh_kernel,
        [VMEM] * 8,
        (
            jax.ShapeDtypeStruct((per_dev, half, 2 * half), jnp.bfloat16),
            jax.ShapeDtypeStruct((per_dev, half, 1), jnp.float32),
            jax.ShapeDtypeStruct((half, width), jnp.float32),
        ),
    )(
        seen_from,
        queries,
        keys,
        with_core(after(keys, seen_from, gate_row)),
        values,
        with_core(values),
        past_keys,
        past_keys_too,
    )
    outs = kernel_call(
        finish_kernel,
        [VMEM] * 6,
        (block(1),) * CHIPS,
    )(
        past_weight,
        total,
        numer,
        gate_row,
        past_values,
        with_core(after(past_values, far)),
    )
    returned = [outs[0]] + [to_chip(outs[1 + route], ROUTES[route][0]) for route in OUT_ORDER]
    out = pl.pallas_call(
        unpack_kernel,
        out_shape=jax.ShapeDtypeStruct((rows, HEADS * HD), jnp.bfloat16),
        in_specs=[VMEM] * CHIPS,
        out_specs=ANY,
        scratch_shapes=[pltpu.SemaphoreType.DMA((CHIPS,))],
    )(*(pltpu.with_memory_space_constraint(part, pltpu.VMEM) for part in returned))
    return out[None]


def solution(mesh):
    by_chip = mesh.shape["seq"] == 2 * CHIPS
    return jax.shard_map(
        chip_body if by_chip else general_body,
        mesh=mesh,
        in_specs=(
            P("stretch", "seq", None),
            P("stretch", "seq", None),
            P("stretch", "seq", None),
            P("stretch"),
            P("stretch"),
            P(),
        ),
        out_specs=P("stretch", "seq", None),
        check_vma=False,
    )
```

```python
import functools
import math

import jax
import jax.numpy as jnp
from jax import lax
from jax.experimental import pallas as pl
from jax.experimental.pallas import tpu as pltpu
from jax.sharding import PartitionSpec as P

HEADS = 32
HD = 128
VMEM = pl.BlockSpec(memory_space=pltpu.VMEM)
SMEM = pl.BlockSpec(memory_space=pltpu.SMEM)
ANY = pl.BlockSpec(memory_space=pl.ANY)
HBM = pl.BlockSpec(memory_space=pltpu.HBM)


def passed_along(block, axis, distance):
    devices = range(lax.axis_size(axis))
    route = [(i - distance, i) for i in devices if i - distance in devices]
    return lax.ppermute(block, axis, route)


def spread(rows, groups, per_dev, blocks):
    count = rows.shape[0]
    arranged = rows.reshape(count, groups, per_dev, HD).transpose(1, 0, 2, 3)
    return jnp.repeat(arranged, blocks, axis=0)


def general_body(query_rows, key_rows, value_rows, cache_from, time_index, gate_table):
    seq_count = lax.axis_size("seq")
    own_count = query_rows.shape[1]
    blocks = max(seq_count // HEADS, 1)
    per_dev = HEADS * blocks // seq_count
    groups = HEADS // per_dev
    part_len = own_count // blocks
    queries = query_rows[0].reshape(blocks, part_len, groups, per_dev, HD).transpose(2, 0, 1, 3, 4)
    queries = queries.reshape(groups * blocks, part_len, per_dev, HD)
    got_query, got_key, got_value = (
        lax.all_to_all(queries, "seq", split_axis=0, concat_axis=1, tiled=True),
        lax.all_to_all(
            spread(key_rows[0], groups, per_dev, blocks),
            "seq",
            split_axis=0,
            concat_axis=1,
            tiled=True,
        ),
        lax.all_to_all(
            spread(value_rows[0], groups, per_dev, blocks),
            "seq",
            split_axis=0,
            concat_axis=1,
            tiled=True,
        ),
    )
    got_past_key, got_past_value = passed_along((got_key, got_value), "stretch", 1)
    head_queries = got_query[0]
    total_tokens = got_key.shape[1]
    position = jnp.arange(total_tokens)
    later = lax.axis_index("stretch") > 0
    past_visible = jnp.logical_and(position >= cache_from[0], later)
    visible = jnp.concatenate([jnp.ones((total_tokens,), bool), past_visible])
    keys_all = jnp.concatenate([got_key[0], got_past_key[0]], 0)
    values_all = jnp.concatenate([got_value[0], got_past_value[0]], 0)
    span = math.gcd(512, 2 * total_tokens)
    count_blocks = 2 * total_tokens // span
    key_blocks = keys_all.reshape(count_blocks, span, per_dev, HD)
    value_blocks = values_all.reshape(count_blocks, span, per_dev, HD)
    visible_blocks = visible.reshape(count_blocks, span)
    query_count = head_queries.shape[0]
    scale = HD ** (-0.5)

    def absorb(carry, packed):
        largest, total, numer = carry
        key_block, value_block, seen = packed
        scores = (
            jnp.einsum("qhd,khd->hqk", head_queries, key_block, preferred_element_type=jnp.float32)
            * scale
        )
        scores = jnp.where(seen[None, None, :], scores, -1e30)
        updated = jnp.maximum(largest, jnp.max(scores, axis=2))
        factor = jnp.exp(largest - updated)
        weights = jnp.where(seen[None, None, :], jnp.exp(scores - updated[:, :, None]), 0.0)
        total = total * factor + jnp.sum(weights, axis=2)
        numer = numer * jnp.transpose(factor)[:, :, None] + jnp.einsum(
            "hqk,khd->qhd",
            weights.astype(jnp.bfloat16),
            value_block,
            preferred_element_type=jnp.float32,
        )
        return ((updated, total, numer), None)

    initial = (
        jnp.full((per_dev, query_count), -1e30, jnp.float32),
        jnp.zeros((per_dev, query_count), jnp.float32),
        jnp.zeros((query_count, per_dev, HD), jnp.float32),
    )
    (largest, total, numer), unused = lax.scan(
        absorb, initial, (key_blocks, value_blocks, visible_blocks)
    )
    attended = (numer / jnp.transpose(total)[:, :, None]).astype(jnp.bfloat16)
    returned = lax.all_to_all(attended[None], "seq", split_axis=1, concat_axis=0, tiled=True)
    tokens_out = returned.reshape(groups, blocks, part_len, per_dev, HD).transpose(1, 2, 0, 3, 4)
    tokens_out = tokens_out.reshape(own_count, HEADS * HD)
    matched = jnp.arange(gate_table.shape[0]) == time_index[0]
    gate_row = jnp.sum(jnp.where(matched[:, None], gate_table, 0.0), axis=0)
    attn_out = (tokens_out.astype(jnp.float32) * gate_row).astype(jnp.bfloat16)[None]
    return attn_out


CHIPS = 4


def following(chip):
    return 2 * (chip & 1) + 1 - (chip >> 1)


def preceding(chip):
    return 2 - 2 * (chip & 1) + (chip >> 1)


def facing(chip):
    return CHIPS - 1 - chip


ROUTES = ((following, preceding), (facing, facing), (preceding, following))
OUT_ORDER = (0, 1, 2)
KEY_ORDER = (1, 0, 2)
VALUE_ORDER = (0, 1, 2)


def span_of(chip, width):
    return pl.ds(pl.multiple_of(chip * width, width), width)


def run_copies(copies):
    for copy in copies:
        copy.start()
    for copy in copies:
        copy.wait()


def pack_kernel(cuts, *refs):
    whole, parts, sems = refs[:3], refs[3:-1], refs[-1]
    rows = whole[0].shape[0]
    width = parts[0].shape[1]
    here = lax.axis_index("seq") // 2
    copies = []
    for part, (index, chips) in zip(parts, cuts):
        for place, chip in enumerate(chips):
            copies.append(
                pltpu.make_async_copy(
                    whole[index].at[:, span_of(chip(here), width)],
                    part.at[pl.ds(place * rows, rows)],
                    sems.at[len(copies)],
                )
            )
    run_copies(copies)


def join_kernel(places, *refs):
    parts, out_ref = refs[:-1], refs[-1]
    rows = out_ref.shape[0] // len(parts)
    for part, (to, place) in zip(parts, places):
        out_ref[pl.ds(to * rows, rows)] = part[pl.ds(place * rows, rows)]


def query_kernel(own_ref, near_ref, far_ref, out_ref):
    rows = own_ref.shape[0]
    chip = lax.axis_index("seq") // 2
    near_place = jnp.where((chip ^ 1) == following(chip), 1, 3)
    out_ref[pl.ds(0, rows)] = own_ref[...]
    out_ref[pl.ds(2 * rows, rows)] = far_ref[pl.ds(rows, rows)]
    out_ref[pl.ds(pl.multiple_of(near_place * rows, rows), rows)] = near_ref[pl.ds(0, rows)]
    out_ref[pl.ds(pl.multiple_of((4 - near_place) * rows, rows), rows)] = far_ref[pl.ds(0, rows)]


def product(left, right, dims):
    return lax.dot_general(left, right, (dims, ((), ())), preferred_element_type=jnp.float32)


def prepare_kernel(cache_ref, time_ref, gate_ref, from_ref, row_ref, sem):
    chip = lax.axis_index("seq") // 2
    copy = pltpu.make_async_copy(
        gate_ref.at[pl.ds(time_ref[0], 1), span_of(chip, row_ref.shape[1])], row_ref, sem
    )
    copy.start()
    tokens = from_ref.shape[1]
    seen_from = jnp.where(lax.axis_index("stretch") > 0, cache_ref[0], tokens)
    from_ref[...] = jnp.full(from_ref.shape, seen_from, jnp.int32)
    copy.wait()


def weigh_kernel(from_ref, *refs):
    queries, refs = refs[0], refs[1:]
    chips = CHIPS
    key_refs, value_refs, past_refs = refs[0:2], refs[2:4], refs[4:6]
    past_value_ref, past_weight_ref, total_ref, numer_ref = refs[6:10]
    half, width = queries.shape
    rows = half // chips
    core = lax.rem(lax.axis_index("seq"), 2)
    chip = lax.axis_index("seq") // 2
    sources = [chip] + [source(chip) for _, source in ROUTES]
    lane = lax.broadcasted_iota(jnp.int32, (1, rows), 1)
    position = jnp.concatenate(
        [
            lane + (source * 2 + (core ^ other)) * rows
            for other in range(2)
            for source in sources
        ],
        axis=1,
    )
    visible = position >= from_ref[...]
    scale = HD ** (-0.5) * math.log2(math.e)

    def scores(head):
        lanes = pl.ds(head * HD, HD)
        query = queries[:, lanes]
        key = jnp.concatenate([ref[:, lanes] for ref in key_refs], axis=0)
        value = jnp.concatenate([ref[:, lanes] for ref in value_refs], axis=0)
        past_key = jnp.concatenate([ref[:, lanes] for ref in past_refs], axis=0)
        own = product(query, key, ((1,), (1,)))
        past = product(query, past_key, ((1,), (1,)))
        return own, past, value

    def mix(head, own, value, past):
        lanes = pl.ds(head * HD, HD)
        here = product(past, past_value_ref[:, lanes], ((1,), (0,)))
        numer_ref[:, lanes] = product(own, value, ((1,), (0,))) + here

    heads = width // HD
    ready, weighed = scores(0), None
    for head in range(heads):
        own, past, value = ready
        if head + 1 < heads:
            ready = scores(head + 1)
        if weighed is not None:
            mix(*weighed)
        past = jnp.where(visible, past, -1e30)
        largest = jnp.max(jnp.maximum(own, past), axis=1, keepdims=True)
        own = jnp.exp2((own - largest) * scale)
        past = jnp.exp2((past - largest) * scale)
        total_ref[head] = jnp.sum(own + past, axis=1, keepdims=True)
        past = past.astype(jnp.bfloat16)
        past_weight_ref[head] = past[:, half:]
        weighed = (head, own.astype(jnp.bfloat16), value, past[:, :half])
    mix(*weighed)


def finish_kernel(past_weight_ref, total_ref, numer_ref, gate_row, *refs):
    past_ref, outs = refs[0], refs[1:]
    rows, width = outs[0].shape
    for head in range(width // HD):
        lanes = pl.ds(head * HD, HD)
        numer = numer_ref[:, lanes] + product(past_weight_ref[head], past_ref[:, lanes], ((1,), (0,)))
        attended = (numer / total_ref[head]).astype(jnp.bfloat16)
        gated = (attended.astype(jnp.float32) * gate_row[:, lanes]).astype(jnp.bfloat16)
        for place in range(CHIPS):
            outs[place][:, lanes] = gated[place * rows:(place + 1) * rows]


def unpack_kernel(*refs):
    parts, out_ref, sems = refs[:-2], refs[-2], refs[-1]
    chip = lax.axis_index("seq") // 2
    width = parts[0].shape[1]
    sources = [chip] + [ROUTES[route][1](chip) for route in OUT_ORDER]
    run_copies(
        [
            pltpu.make_async_copy(part, out_ref.at[:, span_of(source, width)], sems.at[place])
            for place, (part, source) in enumerate(zip(parts, sources))
        ]
    )


def kernel_call(kernel, ins, outs, scratch=(), work=0):
    many = isinstance(outs, tuple)
    call = pl.pallas_call(
        kernel,
        out_shape=jax.tree.map(lambda out: pltpu.VMEM(out.shape, out.dtype), outs),
        in_specs=ins,
        out_specs=(VMEM,) * len(outs) if many else VMEM,
        scratch_shapes=[*scratch],
        cost_estimate=pl.CostEstimate(flops=work, bytes_accessed=0, transcendentals=0),
        compiler_params=pltpu.CompilerParams(vmem_limit_bytes=4 << 20),
    )

    def run(*operands):
        return call(
            *(
                pltpu.with_memory_space_constraint(operand, spec.memory_space)
                if spec in (VMEM, HBM)
                else operand
                for operand, spec in zip(operands, ins)
            )
        )

    return run


def after(value, *others):
    return lax.optimization_barrier((value, others))[0]


def chip_body(query_rows, key_rows, value_rows, cache_from, time_index, gate_table):
    seq = lax.axis_size("seq")
    rows = query_rows.shape[1]
    width = HEADS * HD // CHIPS
    half = CHIPS * rows
    per_dev = width // HD

    def block(count):
        return jax.ShapeDtypeStruct((count * rows, width), jnp.bfloat16)

    def to_chip(part, target):
        return lax.ppermute(part, "seq", [(i, 2 * target(i // 2) + i % 2) for i in range(seq)])

    def with_core(part):
        return lax.ppermute(part, "seq", [(i, i ^ 1) for i in range(seq)])

    def join(parts, places, work=0):
        kernel = functools.partial(join_kernel, places)
        return kernel_call(kernel, [VMEM] * len(parts), block(len(parts)), work=work)(*parts)

    def stay(chip):
        return chip

    def away(step):
        return lambda chip: chip ^ step

    cuts = [(index, (chip,)) for index in range(2) for chip in (stay, *(to for to, _ in ROUTES))]
    cuts += [(2, (stay,)), (2, (away(2),)), (2, (away(1), away(3)))]
    parts = kernel_call(
        functools.partial(pack_kernel, cuts),
        [HBM] * 3,
        tuple(block(len(chips)) for _, chips in cuts),
        scratch=[pltpu.SemaphoreType.DMA((3 * CHIPS,))],
    )(key_rows[0], value_rows[0], query_rows[0])
    key_parts, value_parts, query_parts = parts[:CHIPS], parts[CHIPS:2 * CHIPS], parts[2 * CHIPS:]

    def gathered(parts, order, work=0):
        got = [parts[0]] + [to_chip(parts[1 + route], ROUTES[route][0]) for route in order]
        return join(got, [(0, 0)] + [(1 + route, 0) for route in order], work)

    keys = gathered(key_parts, KEY_ORDER)
    values = gathered(value_parts, VALUE_ORDER)
    past_keys = passed_along(keys, "stretch", 1)
    past_values = passed_along(values, "stretch", 1)
    own_query, two_on, near = query_parts
    near = to_chip(near, away(1))
    far = to_chip(join([after(two_on, values), near], [(0, 0), (1, 1)]), away(2))
    past_keys_too = with_core(past_keys)
    queries = kernel_call(query_kernel, [VMEM] * 3, block(CHIPS))(
        after(own_query, past_keys_too), near, far
    )
    seen_from, gate_row = kernel_call(
        prepare_kernel,
        [SMEM, SMEM, HBM],
        (
            jax.ShapeDtypeStruct((1, 2 * half), jnp.int32),
            jax.ShapeDtypeStruct((1, width), jnp.float32),
        ),
        scratch=[pltpu.SemaphoreType.DMA],
    )(cache_from, time_index, gate_table)
    past_weight, total, numer = kernel_call(
        weigh_kernel,
        [VMEM] * 9,
        (
            jax.ShapeDtypeStruct((per_dev, half, half), jnp.bfloat16),
            jax.ShapeDtypeStruct((per_dev, half, 1), jnp.float32),
            jax.ShapeDtypeStruct((half, width), jnp.float32),
        ),
    )(
        seen_from,
        queries,
        keys,
        with_core(after(keys, seen_from, gate_row)),
        values,
        with_core(values),
        past_keys,
        past_keys_too,
        past_values,
    )
    outs = kernel_call(
        finish_kernel,
        [VMEM] * 5,
        (block(1),) * CHIPS,
    )(
        past_weight,
        total,
        numer,
        gate_row,
        with_core(after(past_values, far)),
    )
    returned = [outs[0]] + [to_chip(outs[1 + route], ROUTES[route][0]) for route in OUT_ORDER]
    out = pl.pallas_call(
        unpack_kernel,
        out_shape=jax.ShapeDtypeStruct((rows, HEADS * HD), jnp.bfloat16),
        in_specs=[VMEM] * CHIPS,
        out_specs=ANY,
        scratch_shapes=[pltpu.SemaphoreType.DMA((CHIPS,))],
    )(*(pltpu.with_memory_space_constraint(part, pltpu.VMEM) for part in returned))
    return out[None]


def solution(mesh):
    by_chip = mesh.shape["seq"] == 2 * CHIPS
    return jax.shard_map(
        chip_body if by_chip else general_body,
        mesh=mesh,
        in_specs=(
            P("stretch", "seq", None),
            P("stretch", "seq", None),
            P("stretch", "seq", None),
            P("stretch"),
            P("stretch"),
            P(),
        ),
        out_specs=P("stretch", "seq", None),
        check_vma=False,
    )
```

```python
import functools
import math

import jax
import jax.numpy as jnp
from jax import lax
from jax.experimental import pallas as pl
from jax.experimental.pallas import tpu as pltpu
from jax.sharding import PartitionSpec as P

HEADS = 32
HD = 128
VMEM = pl.BlockSpec(memory_space=pltpu.VMEM)
SMEM = pl.BlockSpec(memory_space=pltpu.SMEM)
ANY = pl.BlockSpec(memory_space=pl.ANY)
HBM = pl.BlockSpec(memory_space=pltpu.HBM)


def passed_along(block, axis, distance):
    devices = range(lax.axis_size(axis))
    route = [(i - distance, i) for i in devices if i - distance in devices]
    return lax.ppermute(block, axis, route)


def spread(rows, groups, per_dev, blocks):
    count = rows.shape[0]
    arranged = rows.reshape(count, groups, per_dev, HD).transpose(1, 0, 2, 3)
    return jnp.repeat(arranged, blocks, axis=0)


def general_body(query_rows, key_rows, value_rows, cache_from, time_index, gate_table):
    seq_count = lax.axis_size("seq")
    own_count = query_rows.shape[1]
    blocks = max(seq_count // HEADS, 1)
    per_dev = HEADS * blocks // seq_count
    groups = HEADS // per_dev
    part_len = own_count // blocks
    queries = query_rows[0].reshape(blocks, part_len, groups, per_dev, HD).transpose(2, 0, 1, 3, 4)
    queries = queries.reshape(groups * blocks, part_len, per_dev, HD)
    got_query, got_key, got_value = (
        lax.all_to_all(queries, "seq", split_axis=0, concat_axis=1, tiled=True),
        lax.all_to_all(
            spread(key_rows[0], groups, per_dev, blocks),
            "seq",
            split_axis=0,
            concat_axis=1,
            tiled=True,
        ),
        lax.all_to_all(
            spread(value_rows[0], groups, per_dev, blocks),
            "seq",
            split_axis=0,
            concat_axis=1,
            tiled=True,
        ),
    )
    got_past_key, got_past_value = passed_along((got_key, got_value), "stretch", 1)
    head_queries = got_query[0]
    total_tokens = got_key.shape[1]
    position = jnp.arange(total_tokens)
    later = lax.axis_index("stretch") > 0
    past_visible = jnp.logical_and(position >= cache_from[0], later)
    visible = jnp.concatenate([jnp.ones((total_tokens,), bool), past_visible])
    keys_all = jnp.concatenate([got_key[0], got_past_key[0]], 0)
    values_all = jnp.concatenate([got_value[0], got_past_value[0]], 0)
    span = math.gcd(512, 2 * total_tokens)
    count_blocks = 2 * total_tokens // span
    key_blocks = keys_all.reshape(count_blocks, span, per_dev, HD)
    value_blocks = values_all.reshape(count_blocks, span, per_dev, HD)
    visible_blocks = visible.reshape(count_blocks, span)
    query_count = head_queries.shape[0]
    scale = HD ** (-0.5)

    def absorb(carry, packed):
        largest, total, numer = carry
        key_block, value_block, seen = packed
        scores = (
            jnp.einsum("qhd,khd->hqk", head_queries, key_block, preferred_element_type=jnp.float32)
            * scale
        )
        scores = jnp.where(seen[None, None, :], scores, -1e30)
        updated = jnp.maximum(largest, jnp.max(scores, axis=2))
        factor = jnp.exp(largest - updated)
        weights = jnp.where(seen[None, None, :], jnp.exp(scores - updated[:, :, None]), 0.0)
        total = total * factor + jnp.sum(weights, axis=2)
        numer = numer * jnp.transpose(factor)[:, :, None] + jnp.einsum(
            "hqk,khd->qhd",
            weights.astype(jnp.bfloat16),
            value_block,
            preferred_element_type=jnp.float32,
        )
        return ((updated, total, numer), None)

    initial = (
        jnp.full((per_dev, query_count), -1e30, jnp.float32),
        jnp.zeros((per_dev, query_count), jnp.float32),
        jnp.zeros((query_count, per_dev, HD), jnp.float32),
    )
    (largest, total, numer), unused = lax.scan(
        absorb, initial, (key_blocks, value_blocks, visible_blocks)
    )
    attended = (numer / jnp.transpose(total)[:, :, None]).astype(jnp.bfloat16)
    returned = lax.all_to_all(attended[None], "seq", split_axis=1, concat_axis=0, tiled=True)
    tokens_out = returned.reshape(groups, blocks, part_len, per_dev, HD).transpose(1, 2, 0, 3, 4)
    tokens_out = tokens_out.reshape(own_count, HEADS * HD)
    matched = jnp.arange(gate_table.shape[0]) == time_index[0]
    gate_row = jnp.sum(jnp.where(matched[:, None], gate_table, 0.0), axis=0)
    attn_out = (tokens_out.astype(jnp.float32) * gate_row).astype(jnp.bfloat16)[None]
    return attn_out


CHIPS = 4


def following(chip):
    return 2 * (chip & 1) + 1 - (chip >> 1)


def preceding(chip):
    return 2 - 2 * (chip & 1) + (chip >> 1)


def facing(chip):
    return CHIPS - 1 - chip


ROUTES = ((following, preceding), (facing, facing), (preceding, following))
OUT_ORDER = (0, 1, 2)
KEY_ORDER = (1, 0, 2)
VALUE_ORDER = (0, 1, 2)


def span_of(chip, width):
    return pl.ds(pl.multiple_of(chip * width, width), width)


def run_copies(copies):
    for copy in copies:
        copy.start()
    for copy in copies:
        copy.wait()


def pack_kernel(cuts, *refs):
    whole, parts, sems = refs[:3], refs[3:-1], refs[-1]
    rows = whole[0].shape[0]
    width = parts[0].shape[1]
    here = lax.axis_index("seq") // 2
    copies = []
    for part, (index, chips) in zip(parts, cuts):
        for place, chip in enumerate(chips):
            copies.append(
                pltpu.make_async_copy(
                    whole[index].at[:, span_of(chip(here), width)],
                    part.at[pl.ds(place * rows, rows)],
                    sems.at[len(copies)],
                )
            )
    run_copies(copies)


def join_kernel(places, *refs):
    parts, out_ref = refs[:-1], refs[-1]
    rows = out_ref.shape[0] // len(parts)
    for part, (to, place) in zip(parts, places):
        out_ref[pl.ds(to * rows, rows)] = part[pl.ds(place * rows, rows)]


def query_kernel(own_ref, near_ref, far_ref, out_ref):
    rows = own_ref.shape[0]
    chip = lax.axis_index("seq") // 2
    near_place = jnp.where((chip ^ 1) == following(chip), 1, 3)
    out_ref[pl.ds(0, rows)] = own_ref[...]
    out_ref[pl.ds(2 * rows, rows)] = far_ref[pl.ds(rows, rows)]
    out_ref[pl.ds(pl.multiple_of(near_place * rows, rows), rows)] = near_ref[pl.ds(0, rows)]
    out_ref[pl.ds(pl.multiple_of((4 - near_place) * rows, rows), rows)] = far_ref[pl.ds(0, rows)]


def product(left, right, dims):
    return lax.dot_general(left, right, (dims, ((), ())), preferred_element_type=jnp.float32)


def prepare_kernel(cache_ref, time_ref, gate_ref, from_ref, row_ref, sem):
    chip = lax.axis_index("seq") // 2
    copy = pltpu.make_async_copy(
        gate_ref.at[pl.ds(time_ref[0], 1), span_of(chip, row_ref.shape[1])], row_ref, sem
    )
    copy.start()
    tokens = from_ref.shape[1]
    seen_from = jnp.where(lax.axis_index("stretch") > 0, cache_ref[0], tokens)
    from_ref[...] = jnp.full(from_ref.shape, seen_from, jnp.int32)
    copy.wait()


def weigh_kernel(from_ref, *refs):
    queries, refs = refs[0], refs[1:]
    chips = CHIPS
    key_refs, value_refs, past_refs = refs[0:2], refs[2:4], refs[4:6]
    past_value_ref, past_weight_ref, total_ref, numer_ref = refs[6:10]
    half, width = queries.shape
    rows = half // chips
    core = lax.rem(lax.axis_index("seq"), 2)
    chip = lax.axis_index("seq") // 2
    sources = [chip] + [source(chip) for _, source in ROUTES]
    lane = lax.broadcasted_iota(jnp.int32, (1, rows), 1)
    position = jnp.concatenate(
        [
            lane + (source * 2 + (core ^ other)) * rows
            for other in range(2)
            for source in sources
        ],
        axis=1,
    )
    visible = position >= from_ref[...]
    scale = HD ** (-0.5) * math.log2(math.e)

    def scores(head):
        lanes = pl.ds(head * HD, HD)
        query = queries[:, lanes]
        key = jnp.concatenate([ref[:, lanes] for ref in key_refs], axis=0)
        value = jnp.concatenate([ref[:, lanes] for ref in value_refs], axis=0)
        past_key = jnp.concatenate([ref[:, lanes] for ref in past_refs], axis=0)
        own = product(query, key, ((1,), (1,)))
        past = product(query, past_key, ((1,), (1,)))
        return own, past, value

    def mix(head, own, value, past):
        lanes = pl.ds(head * HD, HD)
        here = product(past, past_value_ref[:, lanes], ((1,), (0,)))
        numer_ref[:, lanes] = product(own, value, ((1,), (0,))) + here

    heads = width // HD
    ready, weighed = scores(0), None
    for head in range(heads):
        own, past, value = ready
        if head + 1 < heads:
            ready = scores(head + 1)
        if weighed is not None:
            mix(*weighed)
        past = jnp.where(visible, past, -1e30)
        largest = jnp.max(jnp.maximum(own, past), axis=1, keepdims=True)
        own = jnp.exp2((own - largest) * scale)
        past = jnp.exp2((past - largest) * scale)
        total_ref[head] = jnp.sum(own + past, axis=1, keepdims=True)
        past = past.astype(jnp.bfloat16)
        past_weight_ref[head] = past[:, half:]
        weighed = (head, own.astype(jnp.bfloat16), value, past[:, :half])
    mix(*weighed)


def finish_kernel(past_weight_ref, total_ref, numer_ref, gate_row, *refs):
    past_ref, outs = refs[0], refs[1:]
    rows, width = outs[0].shape
    for head in range(width // HD):
        lanes = pl.ds(head * HD, HD)
        numer = numer_ref[:, lanes] + product(past_weight_ref[head], past_ref[:, lanes], ((1,), (0,)))
        attended = (numer / total_ref[head]).astype(jnp.bfloat16)
        gated = (attended.astype(jnp.float32) * gate_row[:, lanes]).astype(jnp.bfloat16)
        for place in range(CHIPS):
            outs[place][:, lanes] = gated[place * rows:(place + 1) * rows]


def unpack_kernel(*refs):
    parts, out_ref, sems = refs[:-2], refs[-2], refs[-1]
    chip = lax.axis_index("seq") // 2
    width = parts[0].shape[1]
    sources = [chip] + [ROUTES[route][1](chip) for route in OUT_ORDER]
    run_copies(
        [
            pltpu.make_async_copy(
                part.at[pl.ds(piece * 16, 16)],
                out_ref.at[pl.ds(piece * 16, 16), span_of(source, width)],
                sems.at[place, piece],
            )
            for place, (part, source) in enumerate(zip(parts, sources))
            for piece in range(part.shape[0] // 16)
        ]
    )


def kernel_call(kernel, ins, outs, scratch=(), work=0):
    many = isinstance(outs, tuple)
    call = pl.pallas_call(
        kernel,
        out_shape=jax.tree.map(lambda out: pltpu.VMEM(out.shape, out.dtype), outs),
        in_specs=ins,
        out_specs=(VMEM,) * len(outs) if many else VMEM,
        scratch_shapes=[*scratch],
        cost_estimate=pl.CostEstimate(flops=work, bytes_accessed=0, transcendentals=0),
        compiler_params=pltpu.CompilerParams(vmem_limit_bytes=4 << 20),
    )

    def run(*operands):
        return call(
            *(
                pltpu.with_memory_space_constraint(operand, spec.memory_space)
                if spec in (VMEM, HBM)
                else operand
                for operand, spec in zip(operands, ins)
            )
        )

    return run


def after(value, *others):
    return lax.optimization_barrier((value, others))[0]


def chip_body(query_rows, key_rows, value_rows, cache_from, time_index, gate_table):
    seq = lax.axis_size("seq")
    rows = query_rows.shape[1]
    width = HEADS * HD // CHIPS
    half = CHIPS * rows
    per_dev = width // HD

    def block(count):
        return jax.ShapeDtypeStruct((count * rows, width), jnp.bfloat16)

    def to_chip(part, target):
        return lax.ppermute(part, "seq", [(i, 2 * target(i // 2) + i % 2) for i in range(seq)])

    def with_core(part):
        return lax.ppermute(part, "seq", [(i, i ^ 1) for i in range(seq)])

    def join(parts, places, work=0):
        kernel = functools.partial(join_kernel, places)
        return kernel_call(kernel, [VMEM] * len(parts), block(len(parts)), work=work)(*parts)

    def stay(chip):
        return chip

    def away(step):
        return lambda chip: chip ^ step

    cuts = [(index, (chip,)) for index in range(2) for chip in (stay, *(to for to, _ in ROUTES))]
    cuts += [(2, (stay,)), (2, (away(2),)), (2, (away(1), away(3)))]
    parts = kernel_call(
        functools.partial(pack_kernel, cuts),
        [HBM] * 3,
        tuple(block(len(chips)) for _, chips in cuts),
        scratch=[pltpu.SemaphoreType.DMA((3 * CHIPS,))],
    )(key_rows[0], value_rows[0], query_rows[0])
    key_parts, value_parts, query_parts = parts[:CHIPS], parts[CHIPS:2 * CHIPS], parts[2 * CHIPS:]

    def gathered(parts, order, work=0):
        got = [parts[0]] + [to_chip(parts[1 + route], ROUTES[route][0]) for route in order]
        return join(got, [(0, 0)] + [(1 + route, 0) for route in order], work)

    keys = gathered(key_parts, KEY_ORDER)
    values = gathered(value_parts, VALUE_ORDER)
    past_keys = passed_along(keys, "stretch", 1)
    past_values = passed_along(values, "stretch", 1)
    own_query, two_on, near = query_parts
    near = to_chip(near, away(1))
    far = to_chip(join([after(two_on, values), near], [(0, 0), (1, 1)]), away(2))
    past_keys_too = with_core(past_keys)
    queries = kernel_call(query_kernel, [VMEM] * 3, block(CHIPS))(
        after(own_query, past_keys_too), near, far
    )
    seen_from, gate_row = kernel_call(
        prepare_kernel,
        [SMEM, SMEM, HBM],
        (
            jax.ShapeDtypeStruct((1, 2 * half), jnp.int32),
            jax.ShapeDtypeStruct((1, width), jnp.float32),
        ),
        scratch=[pltpu.SemaphoreType.DMA],
    )(cache_from, time_index, gate_table)
    past_weight, total, numer = kernel_call(
        weigh_kernel,
        [VMEM] * 9,
        (
            jax.ShapeDtypeStruct((per_dev, half, half), jnp.bfloat16),
            jax.ShapeDtypeStruct((per_dev, half, 1), jnp.float32),
            jax.ShapeDtypeStruct((half, width), jnp.float32),
        ),
    )(
        seen_from,
        queries,
        keys,
        with_core(after(keys, seen_from, gate_row)),
        values,
        with_core(values),
        past_keys,
        past_keys_too,
        past_values,
    )
    outs = kernel_call(
        finish_kernel,
        [VMEM] * 5,
        (block(1),) * CHIPS,
    )(
        past_weight,
        total,
        numer,
        gate_row,
        with_core(after(past_values, far)),
    )
    returned = [outs[0]] + [to_chip(outs[1 + route], ROUTES[route][0]) for route in OUT_ORDER]
    out = pl.pallas_call(
        unpack_kernel,
        out_shape=jax.ShapeDtypeStruct((rows, HEADS * HD), jnp.bfloat16),
        in_specs=[VMEM] * CHIPS,
        out_specs=ANY,
        scratch_shapes=[pltpu.SemaphoreType.DMA((CHIPS, rows // 16))],
    )(*(pltpu.with_memory_space_constraint(part, pltpu.VMEM) for part in returned))
    return out[None]


def solution(mesh):
    by_chip = mesh.shape["seq"] == 2 * CHIPS
    return jax.shard_map(
        chip_body if by_chip else general_body,
        mesh=mesh,
        in_specs=(
            P("stretch", "seq", None),
            P("stretch", "seq", None),
            P("stretch", "seq", None),
            P("stretch"),
            P("stretch"),
            P(),
        ),
        out_specs=P("stretch", "seq", None),
        check_vma=False,
    )
```

```python
import functools
import math

import jax
import jax.numpy as jnp
from jax import lax
from jax.experimental import pallas as pl
from jax.experimental.pallas import tpu as pltpu
from jax.sharding import PartitionSpec as P

HEADS = 32
HD = 128
VMEM = pl.BlockSpec(memory_space=pltpu.VMEM)
SMEM = pl.BlockSpec(memory_space=pltpu.SMEM)
ANY = pl.BlockSpec(memory_space=pl.ANY)
HBM = pl.BlockSpec(memory_space=pltpu.HBM)


def passed_along(block, axis, distance):
    devices = range(lax.axis_size(axis))
    route = [(i - distance, i) for i in devices if i - distance in devices]
    return lax.ppermute(block, axis, route)


def spread(rows, groups, per_dev, blocks):
    count = rows.shape[0]
    arranged = rows.reshape(count, groups, per_dev, HD).transpose(1, 0, 2, 3)
    return jnp.repeat(arranged, blocks, axis=0)


def general_body(query_rows, key_rows, value_rows, cache_from, time_index, gate_table):
    seq_count = lax.axis_size("seq")
    own_count = query_rows.shape[1]
    blocks = max(seq_count // HEADS, 1)
    per_dev = HEADS * blocks // seq_count
    groups = HEADS // per_dev
    part_len = own_count // blocks
    queries = query_rows[0].reshape(blocks, part_len, groups, per_dev, HD).transpose(2, 0, 1, 3, 4)
    queries = queries.reshape(groups * blocks, part_len, per_dev, HD)
    got_query, got_key, got_value = (
        lax.all_to_all(queries, "seq", split_axis=0, concat_axis=1, tiled=True),
        lax.all_to_all(
            spread(key_rows[0], groups, per_dev, blocks),
            "seq",
            split_axis=0,
            concat_axis=1,
            tiled=True,
        ),
        lax.all_to_all(
            spread(value_rows[0], groups, per_dev, blocks),
            "seq",
            split_axis=0,
            concat_axis=1,
            tiled=True,
        ),
    )
    got_past_key, got_past_value = passed_along((got_key, got_value), "stretch", 1)
    head_queries = got_query[0]
    total_tokens = got_key.shape[1]
    position = jnp.arange(total_tokens)
    later = lax.axis_index("stretch") > 0
    past_visible = jnp.logical_and(position >= cache_from[0], later)
    visible = jnp.concatenate([jnp.ones((total_tokens,), bool), past_visible])
    keys_all = jnp.concatenate([got_key[0], got_past_key[0]], 0)
    values_all = jnp.concatenate([got_value[0], got_past_value[0]], 0)
    span = math.gcd(512, 2 * total_tokens)
    count_blocks = 2 * total_tokens // span
    key_blocks = keys_all.reshape(count_blocks, span, per_dev, HD)
    value_blocks = values_all.reshape(count_blocks, span, per_dev, HD)
    visible_blocks = visible.reshape(count_blocks, span)
    query_count = head_queries.shape[0]
    scale = HD ** (-0.5)

    def absorb(carry, packed):
        largest, total, numer = carry
        key_block, value_block, seen = packed
        scores = (
            jnp.einsum("qhd,khd->hqk", head_queries, key_block, preferred_element_type=jnp.float32)
            * scale
        )
        scores = jnp.where(seen[None, None, :], scores, -1e30)
        updated = jnp.maximum(largest, jnp.max(scores, axis=2))
        factor = jnp.exp(largest - updated)
        weights = jnp.where(seen[None, None, :], jnp.exp(scores - updated[:, :, None]), 0.0)
        total = total * factor + jnp.sum(weights, axis=2)
        numer = numer * jnp.transpose(factor)[:, :, None] + jnp.einsum(
            "hqk,khd->qhd",
            weights.astype(jnp.bfloat16),
            value_block,
            preferred_element_type=jnp.float32,
        )
        return ((updated, total, numer), None)

    initial = (
        jnp.full((per_dev, query_count), -1e30, jnp.float32),
        jnp.zeros((per_dev, query_count), jnp.float32),
        jnp.zeros((query_count, per_dev, HD), jnp.float32),
    )
    (largest, total, numer), unused = lax.scan(
        absorb, initial, (key_blocks, value_blocks, visible_blocks)
    )
    attended = (numer / jnp.transpose(total)[:, :, None]).astype(jnp.bfloat16)
    returned = lax.all_to_all(attended[None], "seq", split_axis=1, concat_axis=0, tiled=True)
    tokens_out = returned.reshape(groups, blocks, part_len, per_dev, HD).transpose(1, 2, 0, 3, 4)
    tokens_out = tokens_out.reshape(own_count, HEADS * HD)
    matched = jnp.arange(gate_table.shape[0]) == time_index[0]
    gate_row = jnp.sum(jnp.where(matched[:, None], gate_table, 0.0), axis=0)
    attn_out = (tokens_out.astype(jnp.float32) * gate_row).astype(jnp.bfloat16)[None]
    return attn_out


CHIPS = 4


def following(chip):
    return 2 * (chip & 1) + 1 - (chip >> 1)


def preceding(chip):
    return 2 - 2 * (chip & 1) + (chip >> 1)


def facing(chip):
    return CHIPS - 1 - chip


ROUTES = ((following, preceding), (facing, facing), (preceding, following))
OUT_ORDER = (2, 0, 1)
KEY_ORDER = (1, 0, 2)
VALUE_ORDER = (0, 1, 2)


def span_of(chip, width):
    return pl.ds(pl.multiple_of(chip * width, width), width)


def run_copies(copies):
    for copy in copies:
        copy.start()
    for copy in copies:
        copy.wait()


def pack_kernel(cuts, *refs):
    whole, parts, sems = refs[:3], refs[3:-1], refs[-1]
    rows = whole[0].shape[0]
    width = parts[0].shape[1]
    here = lax.axis_index("seq") // 2
    copies = []
    for part, (index, chips) in zip(parts, cuts):
        for place, chip in enumerate(chips):
            copies.append(
                pltpu.make_async_copy(
                    whole[index].at[:, span_of(chip(here), width)],
                    part.at[pl.ds(place * rows, rows)],
                    sems.at[len(copies)],
                )
            )
    run_copies(copies)


def join_kernel(places, *refs):
    parts, out_ref = refs[:-1], refs[-1]
    rows = out_ref.shape[0] // len(parts)
    for part, (to, place) in zip(parts, places):
        out_ref[pl.ds(to * rows, rows)] = part[pl.ds(place * rows, rows)]


def query_kernel(own_ref, near_ref, far_ref, out_ref):
    rows = own_ref.shape[0]
    chip = lax.axis_index("seq") // 2
    near_place = jnp.where((chip ^ 1) == following(chip), 1, 3)
    out_ref[pl.ds(0, rows)] = own_ref[...]
    out_ref[pl.ds(2 * rows, rows)] = far_ref[pl.ds(rows, rows)]
    out_ref[pl.ds(pl.multiple_of(near_place * rows, rows), rows)] = near_ref[pl.ds(0, rows)]
    out_ref[pl.ds(pl.multiple_of((4 - near_place) * rows, rows), rows)] = far_ref[pl.ds(0, rows)]


def product(left, right, dims):
    return lax.dot_general(left, right, (dims, ((), ())), preferred_element_type=jnp.float32)


def prepare_kernel(cache_ref, time_ref, gate_ref, from_ref, row_ref, sem):
    chip = lax.axis_index("seq") // 2
    copy = pltpu.make_async_copy(
        gate_ref.at[pl.ds(time_ref[0], 1), span_of(chip, row_ref.shape[1])], row_ref, sem
    )
    copy.start()
    tokens = from_ref.shape[1]
    seen_from = jnp.where(lax.axis_index("stretch") > 0, cache_ref[0], tokens)
    from_ref[...] = jnp.full(from_ref.shape, seen_from, jnp.int32)
    copy.wait()


def weigh_kernel(from_ref, *refs):
    queries, refs = refs[0], refs[1:]
    chips = CHIPS
    key_refs, value_refs, past_refs = refs[0:2], refs[2:4], refs[4:6]
    past_value_ref, past_weight_ref, total_ref, numer_ref = refs[6:10]
    half, width = queries.shape
    rows = half // chips
    core = lax.rem(lax.axis_index("seq"), 2)
    chip = lax.axis_index("seq") // 2
    sources = [chip] + [source(chip) for _, source in ROUTES]
    lane = lax.broadcasted_iota(jnp.int32, (1, rows), 1)
    position = jnp.concatenate(
        [
            lane + (source * 2 + (core ^ other)) * rows
            for other in range(2)
            for source in sources
        ],
        axis=1,
    )
    visible = position >= from_ref[...]
    scale = HD ** (-0.5) * math.log2(math.e)

    def scores(head):
        lanes = pl.ds(head * HD, HD)
        query = queries[:, lanes]
        key = jnp.concatenate([ref[:, lanes] for ref in key_refs], axis=0)
        value = jnp.concatenate([ref[:, lanes] for ref in value_refs], axis=0)
        past_key = jnp.concatenate([ref[:, lanes] for ref in past_refs], axis=0)
        own = product(query, key, ((1,), (1,)))
        past = product(query, past_key, ((1,), (1,)))
        return own, past, value

    def mix(head, own, value, past):
        lanes = pl.ds(head * HD, HD)
        here = product(past, past_value_ref[:, lanes], ((1,), (0,)))
        numer_ref[:, lanes] = product(own, value, ((1,), (0,))) + here

    heads = width // HD
    ready, weighed = scores(0), None
    for head in range(heads):
        own, past, value = ready
        if head + 1 < heads:
            ready = scores(head + 1)
        if weighed is not None:
            mix(*weighed)
        past = jnp.where(visible, past, -1e30)
        largest = jnp.max(jnp.maximum(own, past), axis=1, keepdims=True)
        own = jnp.exp2((own - largest) * scale)
        past = jnp.exp2((past - largest) * scale)
        total_ref[head] = jnp.sum(own + past, axis=1, keepdims=True)
        past = past.astype(jnp.bfloat16)
        past_weight_ref[head] = past[:, half:]
        weighed = (head, own.astype(jnp.bfloat16), value, past[:, :half])
    mix(*weighed)


def finish_kernel(past_weight_ref, total_ref, numer_ref, gate_row, *refs):
    past_ref, outs = refs[0], refs[1:]
    rows, width = outs[0].shape
    for head in range(width // HD):
        lanes = pl.ds(head * HD, HD)
        numer = numer_ref[:, lanes] + product(past_weight_ref[head], past_ref[:, lanes], ((1,), (0,)))
        attended = (numer / total_ref[head]).astype(jnp.bfloat16)
        gated = (attended.astype(jnp.float32) * gate_row[:, lanes]).astype(jnp.bfloat16)
        for place in range(CHIPS):
            outs[place][:, lanes] = gated[place * rows:(place + 1) * rows]


def unpack_kernel(*refs):
    parts, out_ref, sems = refs[:-2], refs[-2], refs[-1]
    chip = lax.axis_index("seq") // 2
    width = parts[0].shape[1]
    sources = [chip] + [ROUTES[route][1](chip) for route in OUT_ORDER]
    run_copies(
        [
            pltpu.make_async_copy(part, out_ref.at[:, span_of(source, width)], sems.at[place])
            for place, (part, source) in enumerate(zip(parts, sources))
        ]
    )


def kernel_call(kernel, ins, outs, scratch=(), work=0):
    many = isinstance(outs, tuple)
    call = pl.pallas_call(
        kernel,
        out_shape=jax.tree.map(lambda out: pltpu.VMEM(out.shape, out.dtype), outs),
        in_specs=ins,
        out_specs=(VMEM,) * len(outs) if many else VMEM,
        scratch_shapes=[*scratch],
        cost_estimate=pl.CostEstimate(flops=work, bytes_accessed=0, transcendentals=0),
        compiler_params=pltpu.CompilerParams(vmem_limit_bytes=4 << 20),
    )

    def run(*operands):
        return call(
            *(
                pltpu.with_memory_space_constraint(operand, spec.memory_space)
                if spec in (VMEM, HBM)
                else operand
                for operand, spec in zip(operands, ins)
            )
        )

    return run


def after(value, *others):
    return lax.optimization_barrier((value, others))[0]


def chip_body(query_rows, key_rows, value_rows, cache_from, time_index, gate_table):
    seq = lax.axis_size("seq")
    rows = query_rows.shape[1]
    width = HEADS * HD // CHIPS
    half = CHIPS * rows
    per_dev = width // HD

    def block(count):
        return jax.ShapeDtypeStruct((count * rows, width), jnp.bfloat16)

    def to_chip(part, target):
        return lax.ppermute(part, "seq", [(i, 2 * target(i // 2) + i % 2) for i in range(seq)])

    def with_core(part):
        return lax.ppermute(part, "seq", [(i, i ^ 1) for i in range(seq)])

    def join(parts, places, work=0):
        kernel = functools.partial(join_kernel, places)
        return kernel_call(kernel, [VMEM] * len(parts), block(len(parts)), work=work)(*parts)

    def stay(chip):
        return chip

    def away(step):
        return lambda chip: chip ^ step

    cuts = [(index, (chip,)) for index in range(2) for chip in (stay, *(to for to, _ in ROUTES))]
    cuts += [(2, (stay,)), (2, (away(2),)), (2, (away(1), away(3)))]
    parts = kernel_call(
        functools.partial(pack_kernel, cuts),
        [HBM] * 3,
        tuple(block(len(chips)) for _, chips in cuts),
        scratch=[pltpu.SemaphoreType.DMA((3 * CHIPS,))],
    )(key_rows[0], value_rows[0], query_rows[0])
    key_parts, value_parts, query_parts = parts[:CHIPS], parts[CHIPS:2 * CHIPS], parts[2 * CHIPS:]

    def gathered(parts, order, work=0):
        got = [parts[0]] + [to_chip(parts[1 + route], ROUTES[route][0]) for route in order]
        return join(got, [(0, 0)] + [(1 + route, 0) for route in order], work)

    keys = gathered(key_parts, KEY_ORDER)
    values = gathered(value_parts, VALUE_ORDER)
    past_keys = passed_along(keys, "stretch", 1)
    past_values = passed_along(values, "stretch", 1)
    own_query, two_on, near = query_parts
    near = to_chip(near, away(1))
    far = to_chip(join([after(two_on, values), near], [(0, 0), (1, 1)]), away(2))
    past_keys_too = with_core(past_keys)
    queries = kernel_call(query_kernel, [VMEM] * 3, block(CHIPS))(
        after(own_query, past_keys_too), near, far
    )
    seen_from, gate_row = kernel_call(
        prepare_kernel,
        [SMEM, SMEM, HBM],
        (
            jax.ShapeDtypeStruct((1, 2 * half), jnp.int32),
            jax.ShapeDtypeStruct((1, width), jnp.float32),
        ),
        scratch=[pltpu.SemaphoreType.DMA],
    )(cache_from, time_index, gate_table)
    past_weight, total, numer = kernel_call(
        weigh_kernel,
        [VMEM] * 9,
        (
            jax.ShapeDtypeStruct((per_dev, half, half), jnp.bfloat16),
            jax.ShapeDtypeStruct((per_dev, half, 1), jnp.float32),
            jax.ShapeDtypeStruct((half, width), jnp.float32),
        ),
    )(
        seen_from,
        queries,
        keys,
        with_core(after(keys, seen_from, gate_row)),
        values,
        with_core(after(values, seen_from, gate_row)),
        past_keys,
        past_keys_too,
        past_values,
    )
    outs = kernel_call(
        finish_kernel,
        [VMEM] * 5,
        (block(1),) * CHIPS,
    )(
        past_weight,
        total,
        numer,
        gate_row,
        with_core(after(past_values, far)),
    )
    returned = [outs[0]] + [to_chip(outs[1 + route], ROUTES[route][0]) for route in OUT_ORDER]
    out = pl.pallas_call(
        unpack_kernel,
        out_shape=jax.ShapeDtypeStruct((rows, HEADS * HD), jnp.bfloat16),
        in_specs=[VMEM] * CHIPS,
        out_specs=ANY,
        scratch_shapes=[pltpu.SemaphoreType.DMA((CHIPS,))],
    )(*(pltpu.with_memory_space_constraint(part, pltpu.VMEM) for part in returned))
    return out[None]


def solution(mesh):
    by_chip = mesh.shape["seq"] == 2 * CHIPS
    return jax.shard_map(
        chip_body if by_chip else general_body,
        mesh=mesh,
        in_specs=(
            P("stretch", "seq", None),
            P("stretch", "seq", None),
            P("stretch", "seq", None),
            P("stretch"),
            P("stretch"),
            P(),
        ),
        out_specs=P("stretch", "seq", None),
        check_vma=False,
    )
```

```python
import functools
import math

import jax
import jax.numpy as jnp
from jax import lax
from jax.experimental import pallas as pl
from jax.experimental.pallas import tpu as pltpu
from jax.sharding import PartitionSpec as P

HEADS = 32
HD = 128
VMEM = pl.BlockSpec(memory_space=pltpu.VMEM)
SMEM = pl.BlockSpec(memory_space=pltpu.SMEM)
ANY = pl.BlockSpec(memory_space=pl.ANY)
HBM = pl.BlockSpec(memory_space=pltpu.HBM)


def passed_along(block, axis, distance):
    devices = range(lax.axis_size(axis))
    route = [(i - distance, i) for i in devices if i - distance in devices]
    return lax.ppermute(block, axis, route)


def spread(rows, groups, per_dev, blocks):
    count = rows.shape[0]
    arranged = rows.reshape(count, groups, per_dev, HD).transpose(1, 0, 2, 3)
    return jnp.repeat(arranged, blocks, axis=0)


def general_body(query_rows, key_rows, value_rows, cache_from, time_index, gate_table):
    seq_count = lax.axis_size("seq")
    own_count = query_rows.shape[1]
    blocks = max(seq_count // HEADS, 1)
    per_dev = HEADS * blocks // seq_count
    groups = HEADS // per_dev
    part_len = own_count // blocks
    queries = query_rows[0].reshape(blocks, part_len, groups, per_dev, HD).transpose(2, 0, 1, 3, 4)
    queries = queries.reshape(groups * blocks, part_len, per_dev, HD)
    got_query, got_key, got_value = (
        lax.all_to_all(queries, "seq", split_axis=0, concat_axis=1, tiled=True),
        lax.all_to_all(
            spread(key_rows[0], groups, per_dev, blocks),
            "seq",
            split_axis=0,
            concat_axis=1,
            tiled=True,
        ),
        lax.all_to_all(
            spread(value_rows[0], groups, per_dev, blocks),
            "seq",
            split_axis=0,
            concat_axis=1,
            tiled=True,
        ),
    )
    got_past_key, got_past_value = passed_along((got_key, got_value), "stretch", 1)
    head_queries = got_query[0]
    total_tokens = got_key.shape[1]
    position = jnp.arange(total_tokens)
    later = lax.axis_index("stretch") > 0
    past_visible = jnp.logical_and(position >= cache_from[0], later)
    visible = jnp.concatenate([jnp.ones((total_tokens,), bool), past_visible])
    keys_all = jnp.concatenate([got_key[0], got_past_key[0]], 0)
    values_all = jnp.concatenate([got_value[0], got_past_value[0]], 0)
    span = math.gcd(512, 2 * total_tokens)
    count_blocks = 2 * total_tokens // span
    key_blocks = keys_all.reshape(count_blocks, span, per_dev, HD)
    value_blocks = values_all.reshape(count_blocks, span, per_dev, HD)
    visible_blocks = visible.reshape(count_blocks, span)
    query_count = head_queries.shape[0]
    scale = HD ** (-0.5)

    def absorb(carry, packed):
        largest, total, numer = carry
        key_block, value_block, seen = packed
        scores = (
            jnp.einsum("qhd,khd->hqk", head_queries, key_block, preferred_element_type=jnp.float32)
            * scale
        )
        scores = jnp.where(seen[None, None, :], scores, -1e30)
        updated = jnp.maximum(largest, jnp.max(scores, axis=2))
        factor = jnp.exp(largest - updated)
        weights = jnp.where(seen[None, None, :], jnp.exp(scores - updated[:, :, None]), 0.0)
        total = total * factor + jnp.sum(weights, axis=2)
        numer = numer * jnp.transpose(factor)[:, :, None] + jnp.einsum(
            "hqk,khd->qhd",
            weights.astype(jnp.bfloat16),
            value_block,
            preferred_element_type=jnp.float32,
        )
        return ((updated, total, numer), None)

    initial = (
        jnp.full((per_dev, query_count), -1e30, jnp.float32),
        jnp.zeros((per_dev, query_count), jnp.float32),
        jnp.zeros((query_count, per_dev, HD), jnp.float32),
    )
    (largest, total, numer), unused = lax.scan(
        absorb, initial, (key_blocks, value_blocks, visible_blocks)
    )
    attended = (numer / jnp.transpose(total)[:, :, None]).astype(jnp.bfloat16)
    returned = lax.all_to_all(attended[None], "seq", split_axis=1, concat_axis=0, tiled=True)
    tokens_out = returned.reshape(groups, blocks, part_len, per_dev, HD).transpose(1, 2, 0, 3, 4)
    tokens_out = tokens_out.reshape(own_count, HEADS * HD)
    matched = jnp.arange(gate_table.shape[0]) == time_index[0]
    gate_row = jnp.sum(jnp.where(matched[:, None], gate_table, 0.0), axis=0)
    attn_out = (tokens_out.astype(jnp.float32) * gate_row).astype(jnp.bfloat16)[None]
    return attn_out


CHIPS = 4


def following(chip):
    return 2 * (chip & 1) + 1 - (chip >> 1)


def preceding(chip):
    return 2 - 2 * (chip & 1) + (chip >> 1)


def facing(chip):
    return CHIPS - 1 - chip


ROUTES = ((following, preceding), (facing, facing), (preceding, following))
OUT_ORDER = (0, 1, 2)
KEY_ORDER = (1, 0, 2)
VALUE_ORDER = (0, 1, 2)


def span_of(chip, width):
    return pl.ds(pl.multiple_of(chip * width, width), width)


def run_copies(copies):
    for copy in copies:
        copy.start()
    for copy in copies:
        copy.wait()


def pack_kernel(cuts, *refs):
    whole, parts, sems = refs[:3], refs[3:-1], refs[-1]
    rows = whole[0].shape[0]
    width = parts[0].shape[1]
    here = lax.axis_index("seq") // 2
    copies = []
    for part, (index, chips) in zip(parts, cuts):
        for place, chip in enumerate(chips):
            for piece in range(0, rows, 16):
                copies.append(
                    pltpu.make_async_copy(
                        whole[index].at[pl.ds(piece, 16), span_of(chip(here), width)],
                        part.at[pl.ds(place * rows + piece, 16)],
                        sems.at[len(copies)],
                    )
                )
    run_copies(copies)


def join_kernel(places, *refs):
    parts, out_ref = refs[:-1], refs[-1]
    rows = out_ref.shape[0] // len(parts)
    for part, (to, place) in zip(parts, places):
        out_ref[pl.ds(to * rows, rows)] = part[pl.ds(place * rows, rows)]


def query_kernel(own_ref, near_ref, far_ref, out_ref):
    rows = own_ref.shape[0]
    chip = lax.axis_index("seq") // 2
    near_place = jnp.where((chip ^ 1) == following(chip), 1, 3)
    out_ref[pl.ds(0, rows)] = own_ref[...]
    out_ref[pl.ds(2 * rows, rows)] = far_ref[pl.ds(rows, rows)]
    out_ref[pl.ds(pl.multiple_of(near_place * rows, rows), rows)] = near_ref[pl.ds(0, rows)]
    out_ref[pl.ds(pl.multiple_of((4 - near_place) * rows, rows), rows)] = far_ref[pl.ds(0, rows)]


def product(left, right, dims):
    return lax.dot_general(left, right, (dims, ((), ())), preferred_element_type=jnp.float32)


def prepare_kernel(cache_ref, time_ref, gate_ref, from_ref, row_ref, sem):
    chip = lax.axis_index("seq") // 2
    copy = pltpu.make_async_copy(
        gate_ref.at[pl.ds(time_ref[0], 1), span_of(chip, row_ref.shape[1])], row_ref, sem
    )
    copy.start()
    tokens = from_ref.shape[1]
    seen_from = jnp.where(lax.axis_index("stretch") > 0, cache_ref[0], tokens)
    from_ref[...] = jnp.full(from_ref.shape, seen_from, jnp.int32)
    copy.wait()


def weigh_kernel(from_ref, *refs):
    queries, refs = refs[0], refs[1:]
    chips = CHIPS
    key_refs, value_refs, past_refs = refs[0:2], refs[2:4], refs[4:6]
    past_value_ref, past_weight_ref, total_ref, numer_ref = refs[6:10]
    half, width = queries.shape
    rows = half // chips
    core = lax.rem(lax.axis_index("seq"), 2)
    chip = lax.axis_index("seq") // 2
    sources = [chip] + [source(chip) for _, source in ROUTES]
    lane = lax.broadcasted_iota(jnp.int32, (1, rows), 1)
    position = jnp.concatenate(
        [
            lane + (source * 2 + (core ^ other)) * rows
            for other in range(2)
            for source in sources
        ],
        axis=1,
    )
    visible = position >= from_ref[...]
    scale = HD ** (-0.5) * math.log2(math.e)

    def scores(head):
        lanes = pl.ds(head * HD, HD)
        query = queries[:, lanes]
        key = jnp.concatenate([ref[:, lanes] for ref in key_refs], axis=0)
        value = jnp.concatenate([ref[:, lanes] for ref in value_refs], axis=0)
        past_key = jnp.concatenate([ref[:, lanes] for ref in past_refs], axis=0)
        own = product(query, key, ((1,), (1,)))
        past = product(query, past_key, ((1,), (1,)))
        return own, past, value

    def mix(head, own, value, past):
        lanes = pl.ds(head * HD, HD)
        here = product(past, past_value_ref[:, lanes], ((1,), (0,)))
        numer_ref[:, lanes] = product(own, value, ((1,), (0,))) + here

    heads = width // HD
    ready, weighed = scores(0), None
    for head in range(heads):
        own, past, value = ready
        if head + 1 < heads:
            ready = scores(head + 1)
        if weighed is not None:
            mix(*weighed)
        past = jnp.where(visible, past, -1e30)
        largest = jnp.max(jnp.maximum(own, past), axis=1, keepdims=True)
        own = jnp.exp2((own - largest) * scale)
        past = jnp.exp2((past - largest) * scale)
        total_ref[head] = jnp.sum(own + past, axis=1, keepdims=True)
        past = past.astype(jnp.bfloat16)
        past_weight_ref[head] = past[:, half:]
        weighed = (head, own.astype(jnp.bfloat16), value, past[:, :half])
    mix(*weighed)


def finish_kernel(past_weight_ref, total_ref, numer_ref, gate_row, *refs):
    past_ref, outs = refs[0], refs[1:]
    rows, width = outs[0].shape
    for head in range(width // HD):
        lanes = pl.ds(head * HD, HD)
        numer = numer_ref[:, lanes] + product(past_weight_ref[head], past_ref[:, lanes], ((1,), (0,)))
        attended = (numer / total_ref[head]).astype(jnp.bfloat16)
        gated = (attended.astype(jnp.float32) * gate_row[:, lanes]).astype(jnp.bfloat16)
        for place in range(CHIPS):
            outs[place][:, lanes] = gated[place * rows:(place + 1) * rows]


def unpack_kernel(*refs):
    parts, out_ref, sems = refs[:-2], refs[-2], refs[-1]
    chip = lax.axis_index("seq") // 2
    width = parts[0].shape[1]
    sources = [chip] + [ROUTES[route][1](chip) for route in OUT_ORDER]
    run_copies(
        [
            pltpu.make_async_copy(part, out_ref.at[:, span_of(source, width)], sems.at[place])
            for place, (part, source) in enumerate(zip(parts, sources))
        ]
    )


def kernel_call(kernel, ins, outs, scratch=(), work=0):
    many = isinstance(outs, tuple)
    call = pl.pallas_call(
        kernel,
        out_shape=jax.tree.map(lambda out: pltpu.VMEM(out.shape, out.dtype), outs),
        in_specs=ins,
        out_specs=(VMEM,) * len(outs) if many else VMEM,
        scratch_shapes=[*scratch],
        cost_estimate=pl.CostEstimate(flops=work, bytes_accessed=0, transcendentals=0),
        compiler_params=pltpu.CompilerParams(vmem_limit_bytes=4 << 20),
    )

    def run(*operands):
        return call(
            *(
                pltpu.with_memory_space_constraint(operand, spec.memory_space)
                if spec in (VMEM, HBM)
                else operand
                for operand, spec in zip(operands, ins)
            )
        )

    return run


def after(value, *others):
    return lax.optimization_barrier((value, others))[0]


def chip_body(query_rows, key_rows, value_rows, cache_from, time_index, gate_table):
    seq = lax.axis_size("seq")
    rows = query_rows.shape[1]
    width = HEADS * HD // CHIPS
    half = CHIPS * rows
    per_dev = width // HD

    def block(count):
        return jax.ShapeDtypeStruct((count * rows, width), jnp.bfloat16)

    def to_chip(part, target):
        return lax.ppermute(part, "seq", [(i, 2 * target(i // 2) + i % 2) for i in range(seq)])

    def with_core(part):
        return lax.ppermute(part, "seq", [(i, i ^ 1) for i in range(seq)])

    def join(parts, places, work=0):
        kernel = functools.partial(join_kernel, places)
        return kernel_call(kernel, [VMEM] * len(parts), block(len(parts)), work=work)(*parts)

    def stay(chip):
        return chip

    def away(step):
        return lambda chip: chip ^ step

    cuts = [(index, (chip,)) for index in range(2) for chip in (stay, *(to for to, _ in ROUTES))]
    cuts += [(2, (stay,)), (2, (away(2),)), (2, (away(1), away(3)))]
    parts = kernel_call(
        functools.partial(pack_kernel, cuts),
        [HBM] * 3,
        tuple(block(len(chips)) for _, chips in cuts),
        scratch=[pltpu.SemaphoreType.DMA((3 * CHIPS * rows // 16,))],
    )(key_rows[0], value_rows[0], query_rows[0])
    key_parts, value_parts, query_parts = parts[:CHIPS], parts[CHIPS:2 * CHIPS], parts[2 * CHIPS:]

    def gathered(parts, order, work=0):
        got = [parts[0]] + [to_chip(parts[1 + route], ROUTES[route][0]) for route in order]
        return join(got, [(0, 0)] + [(1 + route, 0) for route in order], work)

    keys = gathered(key_parts, KEY_ORDER)
    values = gathered(value_parts, VALUE_ORDER)
    past_keys = passed_along(keys, "stretch", 1)
    past_values = passed_along(values, "stretch", 1)
    own_query, two_on, near = query_parts
    near = to_chip(near, away(1))
    far = to_chip(join([after(two_on, values), near], [(0, 0), (1, 1)]), away(2))
    past_keys_too = with_core(past_keys)
    queries = kernel_call(query_kernel, [VMEM] * 3, block(CHIPS))(
        after(own_query, past_keys_too), near, far
    )
    seen_from, gate_row = kernel_call(
        prepare_kernel,
        [SMEM, SMEM, HBM],
        (
            jax.ShapeDtypeStruct((1, 2 * half), jnp.int32),
            jax.ShapeDtypeStruct((1, width), jnp.float32),
        ),
        scratch=[pltpu.SemaphoreType.DMA],
    )(cache_from, time_index, gate_table)
    past_weight, total, numer = kernel_call(
        weigh_kernel,
        [VMEM] * 9,
        (
            jax.ShapeDtypeStruct((per_dev, half, half), jnp.bfloat16),
            jax.ShapeDtypeStruct((per_dev, half, 1), jnp.float32),
            jax.ShapeDtypeStruct((half, width), jnp.float32),
        ),
    )(
        seen_from,
        queries,
        keys,
        with_core(after(keys, seen_from, gate_row)),
        values,
        with_core(values),
        past_keys,
        past_keys_too,
        past_values,
    )
    outs = kernel_call(
        finish_kernel,
        [VMEM] * 5,
        (block(1),) * CHIPS,
    )(
        past_weight,
        total,
        numer,
        gate_row,
        with_core(after(past_values, far)),
    )
    returned = [outs[0]] + [to_chip(outs[1 + route], ROUTES[route][0]) for route in OUT_ORDER]
    out = pl.pallas_call(
        unpack_kernel,
        out_shape=jax.ShapeDtypeStruct((rows, HEADS * HD), jnp.bfloat16),
        in_specs=[VMEM] * CHIPS,
        out_specs=ANY,
        scratch_shapes=[pltpu.SemaphoreType.DMA((CHIPS,))],
    )(*(pltpu.with_memory_space_constraint(part, pltpu.VMEM) for part in returned))
    return out[None]


def solution(mesh):
    by_chip = mesh.shape["seq"] == 2 * CHIPS
    return jax.shard_map(
        chip_body if by_chip else general_body,
        mesh=mesh,
        in_specs=(
            P("stretch", "seq", None),
            P("stretch", "seq", None),
            P("stretch", "seq", None),
            P("stretch"),
            P("stretch"),
            P(),
        ),
        out_specs=P("stretch", "seq", None),
        check_vma=False,
    )
```
